256 devices in a mesh: dp: 2 (over core), cp: 16 (over y_hi, z), tp: 8 (over x, y_lo).
Axes of the slice: x: 4, y: 4 (y_hi: 2, y_lo: 2; y = y_hi * 2 + y_lo), z: 8, core: 2. Of those that a mesh axis runs over, the one named last changes fastest.
Arguments:
- queries: bfloat16 [2, 8192, 64, 128], P('dp', 'cp', 'tp'), may hold values from -5 to 5
- keys: bfloat16 [2, 8192, 8, 128], P('dp', 'cp', 'tp'), may hold values from -5 to 5
- values: bfloat16 [2, 8192, 8, 128], P('dp', 'cp', 'tp'), may hold values from -6 to 6
- output_gradient: bfloat16 [2, 8192, 64, 128], P('dp', 'cp', 'tp'), may hold values from -48 to 48
- lengths: int32 [2, 12], P('dp'), may hold values from 1 to 1024, 8192 in all within a row
Outputs:
- query_grad: bfloat16 [2, 8192, 64, 128], P('dp', 'cp', 'tp')
- key_grad: bfloat16 [2, 8192, 8, 128], P('dp', 'cp', 'tp')
- value_grad: bfloat16 [2, 8192, 8, 128], P('dp', 'cp', 'tp')
- q_bias_grad: float32 [64, 128], P('tp')
The draws below stay inside these ranges and needn't reach their ends.
Inputs may be any that keep to these rules, and one draw needn't show every extreme that they name: Each row holds the lengths of one pack's 12 responses in pack order; they sum to 8192, and the longest is exactly 1024 tokens.
All inputs are finite; a program needn't handle non-finite values.
Results may differ from the reference program's by a relative error of at most 0.0077.
Values may be sent and summed in bfloat16 or wider, within the bound.
No kernel may reach another device: no remote copies, remote signals or barrier semaphores. Data moves between devices by JAX's collectives and lax.ppermute only.
A program may use at most 64 MiB of HBM per device.

```python
import math
import jax
import jax.numpy as jnp
import numpy as np
from jax import lax

QUERY_HEADS = 64
KEY_VALUE_HEADS = 8
HEAD_SIZE = 128
TOK_DEV = 512
REACH = 2
NRESP = 12
PACK_COUNT = 2
PACK_TOKENS = 8192
MOST = 1024


def draw_queries(key, part):
    owned_key = jax.random.fold_in(key, 1)
    drawn_layout = jnp.clip(jax.random.normal(owned_key, (PACK_COUNT, PACK_TOKENS, QUERY_HEADS, HEAD_SIZE), jnp.float32), -5.0, 5.0)
    return drawn_layout.astype(jnp.bfloat16)


def draw_keys(key, part):
    owned_key = jax.random.fold_in(key, 2)
    drawn_layout = jnp.clip(jax.random.normal(owned_key, (PACK_COUNT, PACK_TOKENS, KEY_VALUE_HEADS, HEAD_SIZE), jnp.float32), -5.0, 5.0)
    return drawn_layout.astype(jnp.bfloat16)


def level_of(stream_key, shape, cuts, smallest, high):
    level = 1.0
    for position, parts in cuts:
        draws = jax.random.uniform(jax.random.fold_in(jax.random.fold_in(stream_key, 6), position), (parts,), jnp.float32, smallest / len(cuts), high / len(cuts))
        level = level * jnp.repeat(jnp.exp(draws), shape[position] // parts).reshape((-1,) + (1,) * (len(shape) - 1 - position))
    return level


def profile(count, total, limit, slope):
    loads = [(1 << 20) // math.isqrt(rank ** slope) + 1 for rank in range(2, count + 1)]
    surplus, given = total - limit - (count - 1), [1] * (count - 1)
    while surplus > 0:
        free = [i for i in range(count - 1) if given[i] < limit]
        mass, budget = sum([loads[i] for i in free]), surplus
        for i in free:
            addition = min(limit - given[i], max(1, budget * loads[i] // mass), surplus)
            given[i] = given[i] + addition
            surplus = surplus - addition
    return np.array([limit] + given)


def ragged_sizes(key, count, total, most, skew):
    if count == 2:
        one = jax.random.randint(key, (), max(1, total - most), min(most, total - 1) + 1)
        return jnp.stack([one, total - one])
    tallies = jnp.asarray(profile(count, total, most, skew), jnp.int32)
    couples = (count - 1) // 2
    giver, taker = tallies[1:1 + 2 * couples:2], tallies[2:2 + 2 * couples:2]
    margin = jnp.minimum(giver - 1, most - taker)
    shifted = jax.random.randint(jax.random.fold_in(key, 1), (couples,), 0, 1 << 20) % (margin + 1)
    tallies = tallies.at[1:1 + 2 * couples:2].set(giver - shifted).at[2:2 + 2 * couples:2].set(taker + shifted)
    return tallies[jax.random.permutation(jax.random.fold_in(key, 2), count)]


def bell_draw(key, dims, width, bound, shards=(), kind=jnp.bfloat16):
    drawn = width * jax.random.normal(key, dims, jnp.float32)
    if shards:
        drawn = drawn * level_of(key, dims, shards, -0.22, 0.18)
    return jnp.clip(drawn, -bound, bound).astype(kind)


def setup_inputs(seed: int = 0) -> dict:
    arg_keys = jax.random.split(jax.random.key(seed), 6)
    return {
        "queries": draw_queries(jax.random.fold_in(arg_keys[5], 71), 0),
        "keys": draw_keys(jax.random.fold_in(arg_keys[5], 71), 0),
        "values": bell_draw(arg_keys[2], (PACK_COUNT, PACK_TOKENS, KEY_VALUE_HEADS, HEAD_SIZE), 1.0, 6.0, ((0, 2), (1, 16), (2, 8))),
        "output_gradient": bell_draw(arg_keys[3], (PACK_COUNT, PACK_TOKENS, QUERY_HEADS, HEAD_SIZE), 8.0, 48.0, ((0, 2), (1, 16), (2, 8))),
        "lengths": jax.vmap(lambda own: ragged_sizes(own, NRESP, PACK_TOKENS, MOST, 2))(jax.random.split(arg_keys[4], PACK_COUNT)).reshape((PACK_COUNT, NRESP)).astype(jnp.int32),
    }


NEGATIVE = -1e+30

def doc_index(doc_ends, positions):
    return lax.optimization_barrier(jnp.sum((doc_ends[None, :] <= positions[:, None]).astype(jnp.int32), axis=1))

def pack_grads(queries, keys, values, output_gradient, lengths):
    group_count = QUERY_HEADS // KEY_VALUE_HEADS
    score_scale = 1.0 / math.sqrt(HEAD_SIZE)
    window = (REACH + 1) * TOK_DEV
    blocks = PACK_TOKENS // TOK_DEV
    grouped_query = queries.reshape(PACK_TOKENS, KEY_VALUE_HEADS, group_count, HEAD_SIZE)
    grouped_gradient = output_gradient.reshape(PACK_TOKENS, KEY_VALUE_HEADS, group_count, HEAD_SIZE)
    doc_ends = jnp.cumsum(lengths).astype(jnp.int32)

    def one_block(carry, block):
        key_acc, value_acc = carry
        qstart = (block * TOK_DEV).astype(jnp.int32)
        kstart = jnp.clip(qstart - REACH * TOK_DEV, 0, PACK_TOKENS - window).astype(jnp.int32)
        q_rows = lax.dynamic_slice_in_dim(grouped_query, qstart, TOK_DEV, 0).astype(jnp.float32)
        g_rows = lax.dynamic_slice_in_dim(grouped_gradient, qstart, TOK_DEV, 0).astype(jnp.float32)
        k_rows = lax.dynamic_slice_in_dim(keys, kstart, window, 0).astype(jnp.float32)
        v_rows = lax.dynamic_slice_in_dim(values, kstart, window, 0).astype(jnp.float32)
        qpos = qstart + jnp.arange(TOK_DEV, dtype=jnp.int32)
        kpos = kstart + jnp.arange(window, dtype=jnp.int32)
        visible = (doc_index(doc_ends, qpos)[:, None] == doc_index(doc_ends, kpos)[None, :]) & (kpos[None, :] <= qpos[:, None])
        scores = jnp.einsum('qgcd,kgd->gcqk', q_rows, k_rows) * score_scale
        dprob = jnp.einsum('qgcd,kgd->gcqk', g_rows, v_rows)
        top = lax.optimization_barrier(jnp.max(jnp.where(visible, scores, NEGATIVE), axis=-1))
        expo = jnp.where(visible, jnp.exp(scores - top[..., None]), 0.0)
        total = lax.optimization_barrier(jnp.sum(expo, axis=-1))
        lse = top + jnp.log(total)
        delta = lax.optimization_barrier(jnp.sum(expo * dprob, axis=-1)) / total
        prob = jnp.where(visible, jnp.exp(scores - lse[..., None]), 0.0)
        dscore = lax.optimization_barrier((prob * (dprob - delta[..., None])).astype(jnp.bfloat16))
        prob_rounded = lax.optimization_barrier(prob.astype(jnp.bfloat16))
        dscore_wide = dscore.astype(jnp.float32)
        dq_block = score_scale * jnp.einsum('gcqk,kgd->qgcd', dscore_wide, k_rows)
        dk_window = jnp.einsum('gcqk,qgcd->kgd', dscore_wide, q_rows)
        dv_window = jnp.einsum('gcqk,qgcd->kgd', prob_rounded.astype(jnp.float32), g_rows)
        key_acc = lax.dynamic_update_slice_in_dim(key_acc, lax.dynamic_slice_in_dim(key_acc, kstart, window, 0) + dk_window, kstart, 0)
        value_acc = lax.dynamic_update_slice_in_dim(value_acc, lax.dynamic_slice_in_dim(value_acc, kstart, window, 0) + dv_window, kstart, 0)
        return ((key_acc, value_acc), dq_block.astype(jnp.bfloat16))
    zero_fill = jnp.zeros((PACK_TOKENS, KEY_VALUE_HEADS, HEAD_SIZE), jnp.float32)
    (key_acc, value_acc), dq_blocks = lax.scan(one_block, (zero_fill, zero_fill), jnp.arange(blocks, dtype=jnp.int32))
    query_grad = dq_blocks.reshape(PACK_TOKENS, QUERY_HEADS, HEAD_SIZE)
    key_grad = (score_scale * key_acc).astype(jnp.bfloat16)
    value_grad = value_acc.astype(jnp.bfloat16)
    return (query_grad, key_grad, value_grad)

def reference(queries, keys, values, output_gradient, lengths):
    dq_list, dk_list, dv_list = ([], [], [])
    for pack in range(PACK_COUNT):
        dq_pack, dk_pack, dv_pack = pack_grads(queries[pack], keys[pack], values[pack], output_gradient[pack], lengths[pack])
        dq_list.append(dq_pack)
        dk_list.append(dk_pack)
        dv_list.append(dv_pack)
    query_grad = jnp.stack(dq_list)
    key_grad = jnp.stack(dk_list)
    value_grad = jnp.stack(dv_list)
    q_bias_grad = lax.optimization_barrier(jnp.sum(query_grad.astype(jnp.float32), axis=(0, 1))) / math.sqrt(PACK_COUNT * PACK_TOKENS)
    return (query_grad, key_grad, value_grad, q_bias_grad)
```

```python
import functools
import math

import jax
import jax.numpy as jnp
from jax import lax
from jax.experimental import pallas as pl
from jax.experimental.pallas import tpu as pltpu
from jax.sharding import PartitionSpec as P

NEGATIVE = -1e30
LOG2E = math.log2(math.e)

NT = (((1,), (1,)), ((), ()))
NN = (((1,), (0,)), ((), ()))

ROWS = 512
CHUNK = 256


def dot(a, b, dims):
    return lax.dot_general(a, b, dims, preferred_element_type=jnp.float32)


class Bounds:
    def __init__(self, lengths_ref, tokens, group):
        self.group = group
        first = lax.axis_index("cp") * tokens
        self.begin = -first
        self.ends = []
        end = -first
        for j in range(lengths_ref.shape[1]):
            end = end + lengths_ref[0, j]
            self.ends.append(end)

    def low(self, pos):
        low = jnp.full_like(pos, self.begin)
        for end in self.ends:
            low = jnp.where(end <= pos, end, low)
        return low

    def tile(self, j):
        span = ROWS // self.group
        t0 = j * span
        row = lax.broadcasted_iota(jnp.int32, (1, ROWS), 1)
        pos = t0 + row // self.group
        low0 = jnp.int32(self.begin)
        for end in self.ends:
            low0 = jnp.where(end <= t0, end, low0)
        return t0, t0 + span - 1, low0, pos, self.low(pos)


def visible(start, pos, low):
    key = start + lax.broadcasted_iota(jnp.int32, (CHUNK, ROWS), 0)
    return (key >= low) & (key <= pos)


def rows_of(j):
    return pl.ds(pl.multiple_of(j * ROWS, ROWS), ROWS)


def stats_chunk(scale2, start, pos, low, q, g, k, v, st_ref, rows):
    scores = dot(k, q, NT) * scale2
    dprob = dot(v, g, NT)
    seen = visible(start, pos, low)
    scores = jnp.where(seen, scores, NEGATIVE)
    top_old = st_ref[0:1, rows]
    top = jnp.maximum(top_old, jnp.max(scores, axis=0, keepdims=True))
    expo = jnp.where(seen, jnp.exp2(scores - top), 0.0)
    factor = jnp.exp2(top_old - top)
    st_ref[0:1, rows] = top
    st_ref[1:2, rows] = st_ref[1:2, rows] * factor + jnp.sum(expo, axis=0, keepdims=True)
    st_ref[2:3, rows] = st_ref[2:3, rows] * factor + jnp.sum(expo * dprob, axis=0, keepdims=True)


def grad_chunk(scale2, start, pos, low, q, g, k, v, lse, delta):
    scores = dot(k, q, NT) * scale2
    dprob = dot(v, g, NT)
    prob = jnp.where(visible(start, pos, low), jnp.exp2(scores - lse), 0.0)
    dscore = (prob * (dprob - delta)).astype(jnp.bfloat16)
    return prob.astype(jnp.bfloat16), dscore


def chunks(tokens):
    return [pl.ds(c * CHUNK, CHUNK) for c in range(tokens // CHUNK)]


def stats_kernel(back, group, scale2, len_ref, q_ref, g_ref, k_ref, v_ref, *refs):
    tokens = k_ref.shape[0]
    bounds = Bounds(len_ref, tokens, group)
    if back:
        old_ref, st_ref = refs
        st_ref[...] = old_ref[...]
    else:
        (st_ref,) = refs
        st_ref[0:1, :] = jnp.full((1, st_ref.shape[1]), NEGATIVE, jnp.float32)
        st_ref[1:3, :] = jnp.zeros((2, st_ref.shape[1]), jnp.float32)

    @pl.loop(0, q_ref.shape[0] // ROWS)
    def _(j):
        t0, t1, low0, pos, low = bounds.tile(j)
        rows = rows_of(j)
        for c, keys in enumerate(chunks(tokens)):
            start = c * CHUNK - back * tokens

            @pl.when((low0 < start + CHUNK) & (start <= t1))
            def _():
                stats_chunk(scale2, start, pos, low, q_ref[rows, :], g_ref[rows, :],
                            k_ref[keys, :], v_ref[keys, :], st_ref, rows)


def far_kernel(group, scale2, len_ref, q_ref, g_ref, k_ref, v_ref, st_in, st_ref, d_ref, acc_ref):
    tokens = k_ref.shape[0]
    head = k_ref.shape[1]
    bounds = Bounds(len_ref, tokens, group)
    st_ref[...] = st_in[...]
    acc_ref[...] = jnp.zeros_like(acc_ref)

    @pl.loop(0, q_ref.shape[0] // ROWS)
    def _(j):
        t0, t1, low0, pos, low = bounds.tile(j)
        rows = rows_of(j)
        starts = [c * CHUNK - 2 * tokens for c in range(tokens // CHUNK)]
        for start, keys in zip(starts, chunks(tokens)):

            @pl.when(low0 < start + CHUNK)
            def _():
                stats_chunk(scale2, start, pos, low, q_ref[rows, :], g_ref[rows, :],
                            k_ref[keys, :], v_ref[keys, :], st_ref, rows)

        total = st_ref[1:2, rows]
        st_ref[0:1, rows] = st_ref[0:1, rows] + jnp.log2(total)
        st_ref[1:2, rows] = st_ref[2:3, rows] / total
        for start, keys in zip(starts, chunks(tokens)):

            @pl.when(low0 < start + CHUNK)
            def _():
                q, g = q_ref[rows, :], g_ref[rows, :]
                prob, dscore = grad_chunk(scale2, start, pos, low, q, g, k_ref[keys, :], v_ref[keys, :],
                                          st_ref[0:1, rows], st_ref[1:2, rows])
                acc_ref[keys, 0:head] += dot(dscore, q, NN)
                acc_ref[keys, head:] += dot(prob, g, NN)

    d_ref[...] = acc_ref[...].astype(d_ref.dtype)


def grad_kernel(group, scale, scale2, len_ref, q_ref, g_ref, k0_ref, v0_ref, k1_ref, v1_ref, k2_ref, v2_ref, st_ref,
                dq_ref, d1_ref, d0_ref, bias_ref, kt_ref, dqt_ref, acc_ref, bsum_ref):
    tokens, head = k0_ref.shape
    bounds = Bounds(len_ref, tokens, group)
    acc_ref[...] = jnp.zeros_like(acc_ref)
    d0_ref[...] = jnp.zeros_like(d0_ref)
    bsum_ref[...] = jnp.zeros_like(bsum_ref)
    for b, k_ref in enumerate((k0_ref, k1_ref, k2_ref)):
        kt_ref[b] = k_ref[...].T

    @pl.loop(0, q_ref.shape[0] // ROWS)
    def _(j):
        t0, t1, low0, pos, low = bounds.tile(j)
        rows = rows_of(j)
        dqt_ref[...] = jnp.zeros_like(dqt_ref)
        for back, k_ref, v_ref, sum_ref in ((2, k2_ref, v2_ref, None), (1, k1_ref, v1_ref, acc_ref), (0, k0_ref, v0_ref, d0_ref)):
            for c, keys in enumerate(chunks(tokens)):
                start = c * CHUNK - back * tokens

                @pl.when((low0 < start + CHUNK) & (start <= t1))
                def _():
                    q, g = q_ref[rows, :], g_ref[rows, :]
                    prob, dscore = grad_chunk(scale2, start, pos, low, q, g, k_ref[keys, :], v_ref[keys, :],
                                              st_ref[0:1, rows], st_ref[1:2, rows])
                    if sum_ref is not None:
                        sum_ref[keys, 0:head] += dot(dscore, q, NN)
                        sum_ref[keys, head:] += dot(prob, g, NN)
                    dqt_ref[...] += dot(kt_ref[back, :, keys], dscore, NN)

        dq = (dqt_ref[...].T * scale).astype(dq_ref.dtype)
        dq_ref[rows, :] = dq
        bsum_ref[...] += jnp.sum(dq.astype(jnp.float32).reshape(ROWS // group, group, head), axis=0)

    d1_ref[...] = acc_ref[...].astype(d1_ref.dtype)
    bias_ref[...] = jnp.broadcast_to(bsum_ref[...][None], bias_ref.shape)


SMEM = pl.BlockSpec(memory_space=pltpu.SMEM)
VMEM = pl.BlockSpec(memory_space=pltpu.VMEM)


def call(kernel, args, outs, scratch, flops):
    return pl.pallas_call(
        kernel,
        out_shape=outs,
        in_specs=[SMEM] + [VMEM] * (len(args) - 1),
        out_specs=jax.tree.map(lambda _: VMEM, outs),
        scratch_shapes=scratch,
        compiler_params=pltpu.CompilerParams(vmem_limit_bytes=40 * 1024 * 1024),
        cost_estimate=pl.CostEstimate(flops=flops, bytes_accessed=4 << 20, transcendentals=0),
    )(*args)


def body(queries, keys, values, output_gradient, lengths):
    tokens, heads, head = queries.shape[1:]
    rows = tokens * heads
    cp = lax.axis_size("cp")
    scale = 1.0 / math.sqrt(head)
    scale2 = scale * LOG2E
    q = queries.reshape(rows, head)
    g = output_gradient.reshape(rows, head)
    k0 = keys.reshape(tokens, head)
    v0 = values.reshape(tokens, head)

    def forth(x):
        return lax.ppermute(x, "cp", [(i, i + 1) for i in range(cp - 1)])

    def back(x):
        return lax.ppermute(x, "cp", [(i + 1, i) for i in range(cp - 1)])

    stats = jax.ShapeDtypeStruct((3, rows), jnp.float32)
    pairs = rows * tokens * head * 2
    k1, v1 = forth(k0), forth(v0)
    st = call(functools.partial(stats_kernel, 0, heads, scale2), (lengths, q, g, k0, v0), stats, [], 2 * pairs)
    k2, v2 = forth(k1), forth(v1)
    st = call(functools.partial(stats_kernel, 1, heads, scale2), (lengths, q, g, k1, v1, st), stats, [], 2 * pairs)
    st, far = call(
        functools.partial(far_kernel, heads, scale2),
        (lengths, q, g, k2, v2, st),
        (stats, jax.ShapeDtypeStruct((tokens, 2 * head), jnp.bfloat16)),
        [pltpu.VMEM((tokens, 2 * head), jnp.float32)],
        pairs,
    )
    far = back(far)
    dq, near, own, bias = call(
        functools.partial(grad_kernel, heads, scale, scale2),
        (lengths, q, g, k0, v0, k1, v1, k2, v2, st),
        (
            jax.ShapeDtypeStruct((rows, head), jnp.bfloat16),
            jax.ShapeDtypeStruct((tokens, 2 * head), jnp.bfloat16),
            jax.ShapeDtypeStruct((tokens, 2 * head), jnp.float32),
            jax.ShapeDtypeStruct((lax.axis_size("dp") * cp, heads, head), jnp.float32),
        ),
        [
            pltpu.VMEM((3, head, tokens), jnp.bfloat16),
            pltpu.VMEM((head, ROWS), jnp.float32),
            pltpu.VMEM((tokens, 2 * head), jnp.float32),
            pltpu.VMEM((heads, head), jnp.float32),
        ],
        10 * pairs,
    )
    near = back((near.astype(jnp.float32) + far.astype(jnp.float32)).astype(jnp.bfloat16))
    bias = lax.all_to_all(bias, ("dp", "cp"), 0, 0)
    token_count = lax.axis_size("dp") * cp * tokens
    q_bias_grad = jnp.sum(bias, axis=0) / math.sqrt(token_count)
    total = own + near.astype(jnp.float32)
    key_grad = (scale * total[:, :head]).astype(jnp.bfloat16)
    value_grad = total[:, head:].astype(jnp.bfloat16)
    return (
        dq.reshape(queries.shape),
        key_grad.reshape(keys.shape),
        value_grad.reshape(values.shape),
        q_bias_grad,
    )


def solution(mesh):
    placed = (
        P("dp", "cp", "tp", None),
        P("dp", "cp", "tp", None),
        P("dp", "cp", "tp", None),
        P("dp", "cp", "tp", None),
        P("dp", None),
    )
    return jax.shard_map(
        body,
        mesh=mesh,
        in_specs=placed,
        out_specs=(
            P("dp", "cp", "tp", None),
            P("dp", "cp", "tp", None),
            P("dp", "cp", "tp", None),
            P("tp", None),
        ),
        check_vma=False,
    )
```

```python
import functools
import math

import jax
import jax.numpy as jnp
from jax import lax
from jax.experimental import pallas as pl
from jax.experimental.pallas import tpu as pltpu
from jax.sharding import PartitionSpec as P

NEGATIVE = -1e30
LOG2E = math.log2(math.e)

NT = (((1,), (1,)), ((), ()))
NN = (((1,), (0,)), ((), ()))

ROWS = 2048
CHUNK = 256
FAR_CHUNK = 128


def dot(a, b, dims):
    return lax.dot_general(a, b, dims, preferred_element_type=jnp.float32)


def block_index():
    return lax.axis_index("cp")


def doc_ends(len_ref, tokens):
    end = -block_index() * tokens
    ends = [end]
    for j in range(len_ref.shape[1]):
        end = end + len_ref[0, j]
        ends.append(end)
    return ends


def low_of(ends, pos):
    low = ends[0]
    for end in ends[1:]:
        low = jnp.where(end <= pos, end, low)
    return low


def plan(len_ref, tokens, rows, group, origin, chunk, items_ref):
    ends = doc_ends(len_ref, tokens)
    span = ROWS // group
    count = jnp.int32(0)
    for j in range(rows // ROWS):
        t0, t1 = j * span, (j + 1) * span - 1
        low0, low1 = low_of(ends, jnp.int32(t0)), low_of(ends, jnp.int32(t1))
        begin = jnp.maximum(low0 - origin, 0) // chunk
        end = min((t1 - origin) // chunk + 1, tokens // chunk)

        def put(c, count):
            start = c * chunk + origin
            masked = (low1 > start) | (start + chunk - 1 > t0)
            items_ref[count] = j * 64 + c * 2 + masked.astype(jnp.int32)
            return count + 1

        count = lax.fori_loop(begin, end, put, count)
    return count


def each_item(items_ref, count, chunk, step):
    @pl.loop(0, count)
    def _(i):
        item = items_ref[i]
        rows = pl.ds(pl.multiple_of(item // 64 * ROWS, ROWS), ROWS)
        first = pl.multiple_of((item // 2) % 32 * chunk, chunk)
        keys = pl.ds(first, chunk)

        @pl.when(item % 2 == 1)
        def _():
            step(rows, keys, first, True)

        @pl.when(item % 2 == 0)
        def _():
            step(rows, keys, first, False)


def hide(x, start, rows, see_ref):
    low = see_ref[0:1, rows] - start
    key = lax.broadcasted_iota(jnp.int32, x.shape, 0)
    seen = (key - low).astype(jnp.uint32) <= see_ref[1:2, rows].astype(jnp.uint32)
    return jnp.where(seen, x, NEGATIVE)


def add_stats(scale2, origin, q_ref, g_ref, kv_ref, see_ref, st_ref, rows, keys, first, masked):
    head = q_ref.shape[1]
    scores = dot(kv_ref[keys, 0:head], q_ref[rows, :], NT) * scale2
    dprob = dot(kv_ref[keys, head:], g_ref[rows, :], NT)
    if masked:
        scores = hide(scores, first + origin, rows, see_ref)
    top_old = st_ref[0:1, rows]
    top = jnp.maximum(top_old, jnp.max(scores, axis=0, keepdims=True))
    expo = jnp.exp2(scores - top)
    factor = jnp.exp2(top_old - top)
    st_ref[0:1, rows] = top
    st_ref[1:2, rows] = st_ref[1:2, rows] * factor + jnp.sum(expo, axis=0, keepdims=True)
    st_ref[2:3, rows] = st_ref[2:3, rows] * factor + jnp.sum(expo * dprob, axis=0, keepdims=True)


def add_grads(scale2, origin, q_ref, g_ref, kv_ref, kt_ref, see_ref, st_ref, dqt_ref, sum_ref, rows, keys, first, masked):
    head = q_ref.shape[1]
    q, g = q_ref[rows, :], g_ref[rows, :]
    scores = dot(kv_ref[keys, 0:head], q, NT) * scale2 - st_ref[0:1, rows]
    dprob = dot(kv_ref[keys, head:], g, NT)
    if masked:
        scores = hide(scores, first + origin, rows, see_ref)
    prob = jnp.exp2(scores)
    dscore = (prob * (dprob - st_ref[1:2, rows])).astype(jnp.bfloat16)
    sum_ref[keys, 0:head] += dot(dscore, q, NN)
    sum_ref[keys, head:] += dot(prob.astype(jnp.bfloat16), g, NN)
    dqt_ref[:, rows] += dot(kt_ref[:, keys], dscore, NN)


def own_stats(group, scale2, len_ref, q_hbm, g_hbm, kv_ref, q_ref, g_ref, see_ref, st_ref, items_ref, sems):
    tokens = kv_ref.shape[0]
    fetches = []
    for j in range(q_ref.shape[0] // ROWS):
        rows = pl.ds(j * ROWS, ROWS)
        fetches.append(pltpu.make_async_copy(q_hbm.at[rows, :], q_ref.at[rows, :], sems.at[2 * j]))
        fetches.append(pltpu.make_async_copy(g_hbm.at[rows, :], g_ref.at[rows, :], sems.at[2 * j + 1]))
    for fetch in fetches:
        fetch.start()
    pos = lax.broadcasted_iota(jnp.int32, (1, q_ref.shape[0]), 1) // group
    low = low_of(doc_ends(len_ref, tokens), pos)
    see_ref[0:1, :] = low
    see_ref[1:2, :] = pos - low
    st_ref[0:1, :] = jnp.full((1, st_ref.shape[1]), NEGATIVE, jnp.float32)
    st_ref[1:3, :] = jnp.zeros((2, st_ref.shape[1]), jnp.float32)
    count = plan(len_ref, tokens, q_ref.shape[0], group, 0, CHUNK, items_ref)
    for fetch in fetches:
        fetch.wait()
    each_item(items_ref, count, CHUNK, functools.partial(add_stats, scale2, 0, q_ref, g_ref, kv_ref, see_ref, st_ref))


def near_stats(group, scale2, len_ref, q_ref, g_ref, kv_ref, see_ref, st_in, st_ref, items_ref):
    tokens = kv_ref.shape[0]
    st_ref[...] = st_in[...]
    count = plan(len_ref, tokens, q_ref.shape[0], group, -tokens, CHUNK, items_ref)
    each_item(items_ref, count, CHUNK, functools.partial(add_stats, scale2, -tokens, q_ref, g_ref, kv_ref, see_ref, st_ref))


def far_grads(group, scale2, len_ref, q_ref, g_ref, kv_ref, see_ref, st_in,
              st_ref, far_ref, dqt_ref, run_ref, sum_ref, kt_ref, items_ref):
    tokens = kv_ref.shape[0]
    head = q_ref.shape[1]
    origin = -2 * tokens
    run_ref[...] = st_in[...]
    dqt_ref[...] = jnp.zeros_like(dqt_ref)
    count = plan(len_ref, tokens, q_ref.shape[0], group, origin, FAR_CHUNK, items_ref)
    each_item(items_ref, count, FAR_CHUNK, functools.partial(
        add_stats, scale2, origin, q_ref, g_ref, kv_ref, see_ref, run_ref))
    total = run_ref[1:2, :]
    st_ref[0:1, :] = run_ref[0:1, :] + jnp.log2(total)
    st_ref[1:2, :] = run_ref[2:3, :] / total
    sum_ref[...] = jnp.zeros_like(sum_ref)
    kt_ref[...] = kv_ref[:, 0:head].T
    each_item(items_ref, count, FAR_CHUNK, functools.partial(
        add_grads, scale2, origin, q_ref, g_ref, kv_ref, kt_ref, see_ref, st_ref, dqt_ref, sum_ref))
    far_ref[...] = sum_ref[...].astype(far_ref.dtype)


def main_grads(group, scale, scale2, len_ref, q_ref, g_ref, kv1_ref, kv0_ref, see_ref, st_ref, dqt_in,
               dq_ref, near_ref, own_ref, bias_ref, dqt_ref, kt_ref, items_ref):
    tokens = kv0_ref.shape[0]
    count_rows, head = q_ref.shape
    dqt_ref[...] = dqt_in[...]
    for origin, kv_ref, sum_ref in ((-tokens, kv1_ref, near_ref), (0, kv0_ref, own_ref)):
        sum_ref[...] = jnp.zeros_like(sum_ref)
        kt_ref[...] = kv_ref[:, 0:head].T
        count = plan(len_ref, tokens, count_rows, group, origin, CHUNK, items_ref)
        each_item(items_ref, count, CHUNK, functools.partial(
            add_grads, scale2, origin, q_ref, g_ref, kv_ref, kt_ref, see_ref, st_ref, dqt_ref, sum_ref))

    def finish(j, bias):
        rows = pl.ds(pl.multiple_of(j * ROWS, ROWS), ROWS)
        dq = (dqt_ref[:, rows].T * scale).astype(dq_ref.dtype)
        dq_ref[rows, :] = dq
        return bias + jnp.sum(dq.astype(jnp.float32).reshape(ROWS // group, group, head), axis=0)

    bias = lax.fori_loop(0, count_rows // ROWS, finish, jnp.zeros((group, head), jnp.float32))
    bias_ref[...] = jnp.broadcast_to(bias[None], bias_ref.shape)


def combine(scale, root, own_ref, near_ref, bias_ref, dk_ref, dv_ref, db_ref):
    head = dk_ref.shape[1]
    total = own_ref[...] + near_ref[...].astype(jnp.float32)
    dk_ref[...] = (scale * total[:, :head]).astype(dk_ref.dtype)
    dv_ref[...] = total[:, head:].astype(dv_ref.dtype)
    db_ref[...] = jnp.sum(bias_ref[...], axis=0) / root


SMEM = pl.BlockSpec(memory_space=pltpu.SMEM)
VMEM = pl.BlockSpec(memory_space=pltpu.VMEM)
HBM = pl.BlockSpec(memory_space=pltpu.HBM)


def call(kernel, specs, args, outs, scratch, flops):
    return pl.pallas_call(
        kernel,
        out_shape=outs,
        in_specs=specs,
        out_specs=jax.tree.map(lambda _: VMEM, outs),
        scratch_shapes=scratch,
        compiler_params=pltpu.CompilerParams(vmem_limit_bytes=32 * 1024 * 1024),
        cost_estimate=pl.CostEstimate(flops=flops, bytes_accessed=4 << 20, transcendentals=0),
    )(*args)


def array(dtype, *shape):
    return jax.ShapeDtypeStruct(shape, dtype)


def body(queries, keys, values, output_gradient, lengths):
    tokens, heads, head = queries.shape[1:]
    rows = tokens * heads
    cp = lax.axis_size("cp")
    peers = lax.axis_size("dp") * cp
    scale = 1.0 / math.sqrt(head)
    scale2 = scale * LOG2E
    bf16, f32 = jnp.bfloat16, jnp.float32
    q_hbm = pltpu.with_memory_space_constraint(queries.reshape(rows, head), pltpu.HBM)
    g_hbm = pltpu.with_memory_space_constraint(output_gradient.reshape(rows, head), pltpu.HBM)
    kv0 = jnp.concatenate([keys.reshape(tokens, head), values.reshape(tokens, head)], axis=1)
    items = pltpu.SMEM((64,), jnp.int32)
    pairs = rows * tokens * head * 2

    def shift(x, steps):
        return lax.ppermute(x, "cp", [(i, i + steps) for i in range(max(0, -steps), min(cp, cp - steps))])

    kv1 = shift(kv0, 1)
    q, g, see, st = call(
        functools.partial(own_stats, heads, scale2),
        [SMEM, HBM, HBM, VMEM],
        (lengths, q_hbm, g_hbm, kv0),
        (array(bf16, rows, head), array(bf16, rows, head), array(jnp.int32, 2, rows), array(f32, 3, rows)),
        [items, pltpu.SemaphoreType.DMA((2 * (rows // ROWS),))],
        2 * pairs,
    )
    kv1, st = lax.optimization_barrier((kv1, st))
    kv2 = shift(kv1, 1)
    st = call(
        functools.partial(near_stats, heads, scale2),
        [SMEM] + [VMEM] * 5,
        (lengths, q, g, kv1, see, st),
        array(f32, 3, rows),
        [items],
        2 * pairs,
    )
    st, far, dqt = call(
        functools.partial(far_grads, heads, scale2),
        [SMEM] + [VMEM] * 5,
        (lengths, q, g, kv2, see, st),
        (array(f32, 2, rows), array(bf16, tokens, 2 * head), array(f32, head, rows)),
        [pltpu.VMEM((3, rows), f32), pltpu.VMEM((tokens, 2 * head), f32), pltpu.VMEM((head, tokens), bf16), items],
        pairs,
    )
    far = shift(far, -1)
    dq, near, own, bias = call(
        functools.partial(main_grads, heads, scale, scale2),
        [SMEM] + [VMEM] * 7,
        (lengths, q, g, kv1, kv0, see, st, dqt),
        (array(bf16, rows, head), array(f32, tokens, 2 * head), array(f32, tokens, 2 * head), array(f32, peers, heads, head)),
        [pltpu.VMEM((head, rows), f32), pltpu.VMEM((head, tokens), bf16), items],
        8 * pairs,
    )
    near, bias = lax.optimization_barrier(((near + far.astype(f32)).astype(bf16), bias))
    near = shift(near, -1)
    bias = lax.all_to_all(bias, ("dp", "cp"), 0, 0)
    root = math.sqrt(lax.axis_size("dp") * cp * tokens)
    key_grad, value_grad, q_bias_grad = call(
        functools.partial(combine, scale, root),
        [VMEM] * 3,
        (own, near, bias),
        (array(bf16, tokens, head), array(bf16, tokens, head), array(f32, heads, head)),
        [],
        1000,
    )
    return (
        dq.reshape(queries.shape),
        key_grad.reshape(keys.shape),
        value_grad.reshape(values.shape),
        q_bias_grad,
    )


def solution(mesh):
    placed = (
        P("dp", "cp", "tp", None),
        P("dp", "cp", "tp", None),
        P("dp", "cp", "tp", None),
        P("dp", "cp", "tp", None),
        P("dp", None),
    )
    return jax.shard_map(
        body,
        mesh=mesh,
        in_specs=placed,
        out_specs=(
            P("dp", "cp", "tp", None),
            P("dp", "cp", "tp", None),
            P("dp", "cp", "tp", None),
            P("tp", None),
        ),
        check_vma=False,
    )
```

```python
import functools
import math

import jax
import jax.numpy as jnp
from jax import lax
from jax.experimental import pallas as pl
from jax.experimental.pallas import tpu as pltpu
from jax.sharding import PartitionSpec as P

NEGATIVE = -1e30
LOG2E = math.log2(math.e)

NT = (((1,), (1,)), ((), ()))
NN = (((1,), (0,)), ((), ()))

ROWS = 2048
CHUNK = 256
FAR_CHUNK = 128
VMEM_LIMIT = 12 << 20


def dot(a, b, dims):
    return lax.dot_general(a, b, dims, preferred_element_type=jnp.float32)


def block_index():
    return lax.axis_index("cp")


def doc_ends(len_ref, tokens):
    end = -block_index() * tokens
    ends = [end]
    for j in range(len_ref.shape[1]):
        end = end + len_ref[0, j]
        ends.append(end)
    return ends


def low_of(ends, pos):
    low = ends[0]
    for end in ends[1:]:
        low = jnp.where(end <= pos, end, low)
    return low


def plan(len_ref, tokens, rows, group, origin, chunk, items_ref):
    ends = doc_ends(len_ref, tokens)
    span = ROWS // group
    count = jnp.int32(0)
    for j in range(rows // ROWS):
        t0, t1 = j * span, (j + 1) * span - 1
        low0, low1 = low_of(ends, jnp.int32(t0)), low_of(ends, jnp.int32(t1))
        begin = jnp.maximum(low0 - origin, 0) // chunk
        end = min((t1 - origin) // chunk + 1, tokens // chunk)

        def put(c, count):
            start = c * chunk + origin
            masked = (low1 > start) | (start + chunk - 1 > t0)
            items_ref[count] = j * 64 + c * 2 + masked.astype(jnp.int32)
            return count + 1

        count = lax.fori_loop(begin, end, put, count)
    return count


def each_item(items_ref, count, chunk, step):
    @pl.loop(0, count)
    def _(i):
        item = items_ref[i]
        tile = item // 64
        first = pl.multiple_of((item // 2) % 32 * chunk, chunk)

        @pl.when(item % 2 == 1)
        def _():
            step(tile, first, True)

        @pl.when(item % 2 == 0)
        def _():
            step(tile, first, False)


def tile_rows(tile):
    return pl.ds(pl.multiple_of(tile * ROWS, ROWS), ROWS)


def slot_of(tile, first, origin, tokens):
    before = tile * tokens if origin else tile * (tile + 1) // 2 * CHUNK
    return pl.ds(pl.multiple_of(before + first, CHUNK), CHUNK)


def hide(x, start, rows, see_ref):
    low = see_ref[0:1, rows] - start
    key = lax.broadcasted_iota(jnp.int32, x.shape, 0)
    seen = (key - low).astype(jnp.uint32) <= see_ref[1:2, rows].astype(jnp.uint32)
    return jnp.where(seen, x, NEGATIVE)


def add_stats(scale2, origin, chunk, q_ref, g_ref, kv_ref, see_ref, st_ref, keep, tile, first, masked):
    tokens = kv_ref.shape[0]
    head = q_ref.shape[1]
    rows, keys = tile_rows(tile), pl.ds(first, chunk)
    scores = dot(kv_ref[keys, 0:head], q_ref[rows, :], NT) * scale2
    dprob = dot(kv_ref[keys, head:], g_ref[rows, :], NT)
    if masked:
        scores = hide(scores, first + origin, rows, see_ref)
    if keep:
        slot = slot_of(tile, first, origin, tokens)
        keep[0][slot, :] = scores
        keep[1][slot, :] = dprob
    top_old = st_ref[0:1, rows]
    top = jnp.maximum(top_old, jnp.max(scores, axis=0, keepdims=True))
    expo = jnp.exp2(scores - top)
    factor = jnp.exp2(top_old - top)
    st_ref[0:1, rows] = top
    st_ref[1:2, rows] = st_ref[1:2, rows] * factor + jnp.sum(expo, axis=0, keepdims=True)
    st_ref[2:3, rows] = st_ref[2:3, rows] * factor + jnp.sum(expo * dprob, axis=0, keepdims=True)


def add_grads(scale2, origin, chunk, q_ref, g_ref, kv_ref, kt_ref, see_ref, st_ref, dqt_ref, sum_ref, keep, tile, first, masked):
    tokens = kv_ref.shape[0]
    head = q_ref.shape[1]
    rows, keys = tile_rows(tile), pl.ds(first, chunk)
    q, g = q_ref[rows, :], g_ref[rows, :]
    if keep:
        slot = slot_of(tile, first, origin, tokens)
        scores, dprob = keep[0][slot, :], keep[1][slot, :]
    else:
        scores = dot(kv_ref[keys, 0:head], q, NT) * scale2
        dprob = dot(kv_ref[keys, head:], g, NT)
        if masked:
            scores = hide(scores, first + origin, rows, see_ref)
    prob = jnp.exp2(scores - st_ref[0:1, rows])
    dscore = (prob * (dprob - st_ref[1:2, rows])).astype(jnp.bfloat16)
    sum_ref[keys, 0:head] += dot(dscore, q, NN)
    sum_ref[keys, head:] += dot(prob.astype(jnp.bfloat16), g, NN)
    dqt_ref[:, rows] += dot(kt_ref[:, keys], dscore, NN)


def own_stats(group, scale2, len_ref, q_hbm, g_hbm, kv_ref, q_ref, g_ref, see_ref, st_ref, s_ref, dp_ref, items_ref, sems):
    tokens = kv_ref.shape[0]
    fetches = []
    for j in range(q_ref.shape[0] // ROWS):
        rows = pl.ds(j * ROWS, ROWS)
        fetches.append(pltpu.make_async_copy(q_hbm.at[rows, :], q_ref.at[rows, :], sems.at[2 * j]))
        fetches.append(pltpu.make_async_copy(g_hbm.at[rows, :], g_ref.at[rows, :], sems.at[2 * j + 1]))
    for fetch in fetches:
        fetch.start()
    pos = lax.broadcasted_iota(jnp.int32, (1, q_ref.shape[0]), 1) // group
    low = low_of(doc_ends(len_ref, tokens), pos)
    see_ref[0:1, :] = low
    see_ref[1:2, :] = pos - low
    st_ref[0:1, :] = jnp.full((1, st_ref.shape[1]), NEGATIVE, jnp.float32)
    st_ref[1:3, :] = jnp.zeros((2, st_ref.shape[1]), jnp.float32)
    count = plan(len_ref, tokens, q_ref.shape[0], group, 0, CHUNK, items_ref)
    for fetch in fetches:
        fetch.wait()
    each_item(items_ref, count, CHUNK, functools.partial(
        add_stats, scale2, 0, CHUNK, q_ref, g_ref, kv_ref, see_ref, st_ref, (s_ref, dp_ref)))


def near_stats(group, scale2, len_ref, q_ref, g_ref, kv_ref, see_ref, st_in, st_ref, s_ref, dp_ref, items_ref):
    tokens = kv_ref.shape[0]
    st_ref[...] = st_in[...]
    count = plan(len_ref, tokens, q_ref.shape[0], group, -tokens, CHUNK, items_ref)
    each_item(items_ref, count, CHUNK, functools.partial(
        add_stats, scale2, -tokens, CHUNK, q_ref, g_ref, kv_ref, see_ref, st_ref, (s_ref, dp_ref)))


def far_grads(group, scale2, len_ref, q_ref, g_ref, kv_ref, see_ref, st_in,
              st_ref, far_ref, dqt_ref, run_ref, sum_ref, kt_ref, items_ref):
    tokens = kv_ref.shape[0]
    head = q_ref.shape[1]
    origin = -2 * tokens
    run_ref[...] = st_in[...]
    dqt_ref[...] = jnp.zeros_like(dqt_ref)
    count = plan(len_ref, tokens, q_ref.shape[0], group, origin, FAR_CHUNK, items_ref)
    each_item(items_ref, count, FAR_CHUNK, functools.partial(
        add_stats, scale2, origin, FAR_CHUNK, q_ref, g_ref, kv_ref, see_ref, run_ref, None))
    total = run_ref[1:2, :]
    st_ref[0:1, :] = run_ref[0:1, :] + jnp.log2(total)
    st_ref[1:2, :] = run_ref[2:3, :] / total
    sum_ref[...] = jnp.zeros_like(sum_ref)
    kt_ref[...] = kv_ref[:, 0:head].T
    each_item(items_ref, count, FAR_CHUNK, functools.partial(
        add_grads, scale2, origin, FAR_CHUNK, q_ref, g_ref, kv_ref, kt_ref, see_ref, st_ref, dqt_ref, sum_ref, None))
    far_ref[...] = sum_ref[...].astype(far_ref.dtype)


def main_grads(group, scale, scale2, len_ref, q_ref, g_ref, kv1_ref, kv0_ref, s1_ref, dp1_ref, s0_ref, dp0_ref, st_ref, dqt_in,
               dq_ref, near_ref, own_ref, bias_ref, dqt_ref, kt_ref, items_ref):
    tokens = kv0_ref.shape[0]
    count_rows, head = q_ref.shape
    dqt_ref[...] = dqt_in[...]
    for origin, kv_ref, sum_ref, keep in (
        (-tokens, kv1_ref, near_ref, (s1_ref, dp1_ref)),
        (0, kv0_ref, own_ref, (s0_ref, dp0_ref)),
    ):
        sum_ref[...] = jnp.zeros_like(sum_ref)
        kt_ref[...] = kv_ref[:, 0:head].T
        count = plan(len_ref, tokens, count_rows, group, origin, CHUNK, items_ref)
        each_item(items_ref, count, CHUNK, functools.partial(
            add_grads, scale2, origin, CHUNK, q_ref, g_ref, kv_ref, kt_ref, None, st_ref, dqt_ref, sum_ref, keep))

    def finish(j, bias):
        rows = pl.ds(pl.multiple_of(j * ROWS, ROWS), ROWS)
        dq = (dqt_ref[:, rows] * scale).astype(dq_ref.dtype).T
        dq_ref[rows, :] = dq
        return bias + jnp.sum(dq.astype(jnp.float32).reshape(ROWS // group, group, head), axis=0)

    bias = lax.fori_loop(0, count_rows // ROWS, finish, jnp.zeros((group, head), jnp.float32))
    bias_ref[...] = jnp.broadcast_to(bias[None], bias_ref.shape)


def combine(scale, root, own_ref, near_ref, bias_ref, dk_ref, dv_ref, db_ref):
    head = dk_ref.shape[1]
    total = own_ref[...] + near_ref[...].astype(jnp.float32)
    dk_ref[...] = (scale * total[:, :head]).astype(dk_ref.dtype)
    dv_ref[...] = total[:, head:].astype(dv_ref.dtype)
    db_ref[...] = jnp.sum(bias_ref[...], axis=0) / root


SMEM = pl.BlockSpec(memory_space=pltpu.SMEM)
VMEM = pl.BlockSpec(memory_space=pltpu.VMEM)
HBM = pl.BlockSpec(memory_space=pltpu.HBM)


def call(kernel, specs, args, outs, scratch, flops):
    return pl.pallas_call(
        kernel,
        out_shape=outs,
        in_specs=specs,
        out_specs=jax.tree.map(lambda _: VMEM, outs),
        scratch_shapes=scratch,
        compiler_params=pltpu.CompilerParams(vmem_limit_bytes=VMEM_LIMIT),
        cost_estimate=pl.CostEstimate(flops=flops, bytes_accessed=4 << 20, transcendentals=0),
    )(*args)


def array(dtype, *shape):
    return jax.ShapeDtypeStruct(shape, dtype)


def body(queries, keys, values, output_gradient, lengths):
    tokens, heads, head = queries.shape[1:]
    rows = tokens * heads
    cp = lax.axis_size("cp")
    peers = lax.axis_size("dp") * cp
    scale = 1.0 / math.sqrt(head)
    scale2 = scale * LOG2E
    bf16, f32 = jnp.bfloat16, jnp.float32
    q_hbm = pltpu.with_memory_space_constraint(queries.reshape(rows, head), pltpu.HBM)
    g_hbm = pltpu.with_memory_space_constraint(output_gradient.reshape(rows, head), pltpu.HBM)
    kv0 = jnp.concatenate([keys.reshape(tokens, head), values.reshape(tokens, head)], axis=1)
    items = pltpu.SMEM((64,), jnp.int32)
    pairs = rows * tokens * head * 2

    def shift(x, steps):
        return lax.ppermute(x, "cp", [(i, i + steps) for i in range(max(0, -steps), min(cp, cp - steps))])

    tiles = rows // ROWS
    kept1 = (array(f32, tiles * tokens, ROWS),) * 2
    kept0 = (array(f32, tiles * (tiles + 1) // 2 * CHUNK, ROWS),) * 2
    kv1 = shift(kv0, 1)
    q, g, see, st, s0, dp0 = call(
        functools.partial(own_stats, heads, scale2),
        [SMEM, HBM, HBM, VMEM],
        (lengths, q_hbm, g_hbm, kv0),
        (array(bf16, rows, head), array(bf16, rows, head), array(jnp.int32, 2, rows), array(f32, 3, rows), *kept0),
        [items, pltpu.SemaphoreType.DMA((2 * (rows // ROWS),))],
        2 * pairs,
    )
    kv1, st = lax.optimization_barrier((kv1, st))
    kv2 = shift(kv1, 1)
    st, s1, dp1 = call(
        functools.partial(near_stats, heads, scale2),
        [SMEM] + [VMEM] * 5,
        (lengths, q, g, kv1, see, st),
        (array(f32, 3, rows), *kept1),
        [items],
        2 * pairs,
    )
    st, far, dqt = call(
        functools.partial(far_grads, heads, scale2),
        [SMEM] + [VMEM] * 5,
        (lengths, q, g, kv2, see, st),
        (array(f32, 2, rows), array(bf16, tokens, 2 * head), array(f32, head, rows)),
        [pltpu.VMEM((3, rows), f32), pltpu.VMEM((tokens, 2 * head), f32), pltpu.VMEM((head, tokens), bf16), items],
        pairs,
    )
    far = shift(far, -1)
    dq, near, own, bias = call(
        functools.partial(main_grads, heads, scale, scale2),
        [SMEM] + [VMEM] * 10,
        (lengths, q, g, kv1, kv0, s1, dp1, s0, dp0, st, dqt),
        (array(bf16, rows, head), array(f32, tokens, 2 * head), array(f32, tokens, 2 * head), array(f32, peers, heads, head)),
        [pltpu.VMEM((head, rows), f32), pltpu.VMEM((head, tokens), bf16), items],
        8 * pairs,
    )
    near, bias = lax.optimization_barrier(((near + far.astype(f32)).astype(bf16), bias))
    near = shift(near, -1)
    bias = lax.all_to_all(bias, ("dp", "cp"), 0, 0)
    root = math.sqrt(lax.axis_size("dp") * cp * tokens)
    key_grad, value_grad, q_bias_grad = call(
        functools.partial(combine, scale, root),
        [VMEM] * 3,
        (own, near, bias),
        (array(bf16, tokens, head), array(bf16, tokens, head), array(f32, heads, head)),
        [],
        1000,
    )
    return (
        dq.reshape(queries.shape),
        key_grad.reshape(keys.shape),
        value_grad.reshape(values.shape),
        q_bias_grad,
    )


def solution(mesh):
    placed = (
        P("dp", "cp", "tp", None),
        P("dp", "cp", "tp", None),
        P("dp", "cp", "tp", None),
        P("dp", "cp", "tp", None),
        P("dp", None),
    )
    return jax.shard_map(
        body,
        mesh=mesh,
        in_specs=placed,
        out_specs=(
            P("dp", "cp", "tp", None),
            P("dp", "cp", "tp", None),
            P("dp", "cp", "tp", None),
            P("tp", None),
        ),
        check_vma=False,
    )
```

```python
import functools
import math

import jax
import jax.numpy as jnp
from jax import lax
from jax.experimental import pallas as pl
from jax.experimental.pallas import tpu as pltpu
from jax.sharding import PartitionSpec as P

NEGATIVE = -1e30
LOG2E = math.log2(math.e)

NT = (((1,), (1,)), ((), ()))
NN = (((1,), (0,)), ((), ()))

ROWS = 2048
CHUNK = 256
FAR_CHUNK = 128
VMEM_LIMIT = 20 << 20
MOST_ITEMS = 32
FAR_SLOTS = 4


def dot(a, b, dims):
    return lax.dot_general(a, b, dims, preferred_element_type=jnp.float32)


def block_index():
    return lax.axis_index("cp")


def doc_ends(len_ref, tokens):
    end = -block_index() * tokens
    ends = [end]
    for j in range(len_ref.shape[1]):
        end = end + len_ref[0, j]
        ends.append(end)
    return ends


def low_of(ends, pos):
    low = ends[0]
    for end in ends[1:]:
        low = jnp.where(end <= pos, end, low)
    return low


def plan(len_ref, tokens, rows, group, origin, chunk, items_ref):
    ends = doc_ends(len_ref, tokens)
    span = ROWS // group
    count = jnp.int32(0)
    for j in range(rows // ROWS):
        items_ref[MOST_ITEMS + j] = count
        t0, t1 = j * span, (j + 1) * span - 1
        low0, low1 = low_of(ends, jnp.int32(t0)), low_of(ends, jnp.int32(t1))
        begin = jnp.maximum(low0 - origin, 0) // chunk
        end = min((t1 - origin) // chunk + 1, tokens // chunk)

        def put(c, count):
            start = c * chunk + origin
            masked = (low1 > start) | (start + chunk - 1 > t0)
            items_ref[count] = j * 64 + c * 2 + masked.astype(jnp.int32)
            return count + 1

        count = lax.fori_loop(begin, end, put, count)
    return count


def each_item(items_ref, begin, end, chunk, step):
    @pl.loop(begin, end)
    def _(i):
        item = items_ref[i]
        tile = item // 64
        first = pl.multiple_of((item // 2) % 32 * chunk, chunk)

        @pl.when(item % 2 == 1)
        def _():
            step(i, tile, first, True)

        @pl.when(item % 2 == 0)
        def _():
            step(i, tile, first, False)


def each_kept(items_ref, begin, end, chunk, step):
    @pl.loop(begin, end)
    def _(i):
        item = items_ref[i]
        step(i, item // 64, pl.multiple_of((item // 2) % 32 * chunk, chunk))


def tile_rows(tile):
    return pl.ds(pl.multiple_of(tile * ROWS, ROWS), ROWS)


def early_slot(i, tile, first):
    return pl.ds(0, CHUNK)


def own_slot(i, tile, first):
    return pl.ds(pl.multiple_of((tile * (tile + 1) // 2 - 1) * CHUNK + first, CHUNK), CHUNK)


def near_slot(tokens, i, tile, first):
    return pl.ds(pl.multiple_of(tile * tokens + first, CHUNK), CHUNK)


def far_slot(i, tile, first):
    return pl.ds(pl.multiple_of(i * FAR_CHUNK, FAR_CHUNK), FAR_CHUNK)


def hide(x, start, rows, see_ref):
    low = see_ref[0:1, rows] - start
    key = lax.broadcasted_iota(jnp.int32, x.shape, 0)
    seen = (key - low).astype(jnp.uint32) <= see_ref[1:2, rows].astype(jnp.uint32)
    return jnp.where(seen, x, NEGATIVE)


def add_stats(scale2, origin, chunk, q_ref, g_ref, k_ref, v_ref, see_ref, st_ref, s_ref, dp_ref, slot_of, i, tile, first, masked):
    rows, keys, slot = tile_rows(tile), pl.ds(first, chunk), slot_of(i, tile, first)
    scores = dot(k_ref[keys, :], q_ref[rows, :], NT) * scale2
    dprob = dot(v_ref[keys, :], g_ref[rows, :], NT)
    if masked:
        scores = hide(scores, first + origin, rows, see_ref)
    s_ref[slot, :] = scores
    dp_ref[slot, :] = dprob
    top_old = st_ref[0:1, rows]
    top = jnp.maximum(top_old, jnp.max(scores, axis=0, keepdims=True))
    expo = jnp.exp2(scores - top)
    factor = jnp.exp2(top_old - top)
    st_ref[0:1, rows] = top
    st_ref[1:2, rows] = st_ref[1:2, rows] * factor + jnp.sum(expo, axis=0, keepdims=True)
    st_ref[2:3, rows] = st_ref[2:3, rows] * factor + jnp.sum(expo * dprob, axis=0, keepdims=True)


def add_grads(chunk, q_ref, g_ref, kt_ref, st_ref, dqt_ref, sum_ref, s_ref, dp_ref, slot_of, i, tile, first):
    head = q_ref.shape[1]
    rows, keys, slot = tile_rows(tile), pl.ds(first, chunk), slot_of(i, tile, first)
    prob = jnp.exp2(s_ref[slot, :] - st_ref[0:1, rows])
    dscore = (prob * (dp_ref[slot, :] - st_ref[1:2, rows])).astype(jnp.bfloat16)
    sum_ref[keys, 0:head] += dot(dscore, q_ref[rows, :], NN)
    sum_ref[keys, head:] += dot(prob.astype(jnp.bfloat16), g_ref[rows, :], NN)
    dqt_ref[:, rows] += dot(kt_ref[:, keys], dscore, NN)


def early_stats(group, scale2, len_ref, q_hbm, g_hbm, k_hbm, v_hbm, q_ref, g_ref, k_ref, v_ref, see_ref, st_ref, s_ref, dp_ref,
                items_ref, sems):
    tokens = k_ref.shape[0]
    count_rows = q_ref.shape[0]
    fetches = [
        pltpu.make_async_copy(source, target, sems.at[n])
        for n, (source, target) in enumerate((
            (k_hbm, k_ref),
            (q_hbm.at[0:ROWS, :], q_ref.at[0:ROWS, :]),
            (v_hbm, v_ref),
            (g_hbm.at[0:ROWS, :], g_ref.at[0:ROWS, :]),
            (q_hbm.at[ROWS:, :], q_ref.at[ROWS:, :]),
            (g_hbm.at[ROWS:, :], g_ref.at[ROWS:, :]),
        ))
    ]
    for fetch in fetches:
        fetch.start()
    pos = lax.broadcasted_iota(jnp.int32, (1, count_rows), 1) // group
    low = low_of(doc_ends(len_ref, tokens), pos)
    see_ref[0:1, :] = low
    see_ref[1:2, :] = pos - low
    st_ref[0:1, :] = jnp.full((1, count_rows), NEGATIVE, jnp.float32)
    st_ref[1:3, :] = jnp.zeros((2, count_rows), jnp.float32)
    for fetch in fetches[:4]:
        fetch.wait()
    add_stats(scale2, 0, CHUNK, q_ref, g_ref, k_ref, v_ref, see_ref, st_ref, s_ref, dp_ref, early_slot, 0, 0, 0, True)
    for fetch in fetches[4:]:
        fetch.wait()


def near_stats(group, scale2, len_ref, q_ref, g_ref, k0_ref, v0_ref, k1_ref, v1_ref, see_ref, st_in,
               st_ref, s0_ref, dp0_ref, s1_ref, dp1_ref, items_ref):
    tokens = k0_ref.shape[0]
    st_ref[...] = st_in[...]
    count = plan(len_ref, tokens, q_ref.shape[0], group, 0, CHUNK, items_ref)
    each_item(items_ref, items_ref[MOST_ITEMS + 1], count, CHUNK, functools.partial(
        add_stats, scale2, 0, CHUNK, q_ref, g_ref, k0_ref, v0_ref, see_ref, st_ref, s0_ref, dp0_ref, own_slot))
    count = plan(len_ref, tokens, q_ref.shape[0], group, -tokens, CHUNK, items_ref)
    each_item(items_ref, 0, count, CHUNK, functools.partial(
        add_stats, scale2, -tokens, CHUNK, q_ref, g_ref, k1_ref, v1_ref, see_ref, st_ref, s1_ref, dp1_ref,
        functools.partial(near_slot, tokens)))


def far_grads(group, scale2, len_ref, q_ref, g_ref, kv_ref, see_ref, st_in,
              st_ref, far_ref, dqt_ref, run_ref, sum_ref, kt_ref, s_ref, dp_ref, items_ref):
    tokens = kv_ref.shape[0]
    head = q_ref.shape[1]
    k_ref, v_ref = kv_ref.at[:, 0:head], kv_ref.at[:, head:]
    origin = -2 * tokens
    run_ref[...] = st_in[...]
    dqt_ref[...] = jnp.zeros_like(dqt_ref)
    sum_ref[...] = jnp.zeros_like(sum_ref)
    kt_ref[...] = k_ref[...].T
    count = plan(len_ref, tokens, q_ref.shape[0], group, origin, FAR_CHUNK, items_ref)
    each_item(items_ref, 0, count, FAR_CHUNK, functools.partial(
        add_stats, scale2, origin, FAR_CHUNK, q_ref, g_ref, k_ref, v_ref, see_ref, run_ref, s_ref, dp_ref, far_slot))
    total = run_ref[1:2, :]
    st_ref[0:1, :] = run_ref[0:1, :] + jnp.log2(total)
    st_ref[1:2, :] = run_ref[2:3, :] / total
    each_kept(items_ref, 0, count, FAR_CHUNK, functools.partial(
        add_grads, FAR_CHUNK, q_ref, g_ref, kt_ref, st_ref, dqt_ref, sum_ref, s_ref, dp_ref, far_slot))
    far_ref[...] = sum_ref[...].astype(far_ref.dtype)


def main_grads(group, scale, len_ref, q_ref, g_ref, k1_ref, k0_ref, s1_ref, dp1_ref, se_ref, dpe_ref, s0_ref, dp0_ref,
               st_ref, dqt_in, dq_ref, near_ref, own_ref, bias_ref, dqt_ref, kt_ref, items_ref):
    tokens = k0_ref.shape[0]
    count_rows, head = q_ref.shape
    dqt_ref[...] = dqt_in[...]
    near_ref[...] = jnp.zeros_like(near_ref)
    kt_ref[...] = k1_ref[...].T
    count = plan(len_ref, tokens, count_rows, group, -tokens, CHUNK, items_ref)
    each_kept(items_ref, 0, count, CHUNK, functools.partial(
        add_grads, CHUNK, q_ref, g_ref, kt_ref, st_ref, dqt_ref, near_ref, s1_ref, dp1_ref, functools.partial(near_slot, tokens)))
    own_ref[...] = jnp.zeros_like(own_ref)
    kt_ref[...] = k0_ref[...].T
    count = plan(len_ref, tokens, count_rows, group, 0, CHUNK, items_ref)
    add_grads(CHUNK, q_ref, g_ref, kt_ref, st_ref, dqt_ref, own_ref, se_ref, dpe_ref, early_slot, 0, 0, 0)
    each_kept(items_ref, items_ref[MOST_ITEMS + 1], count, CHUNK, functools.partial(
        add_grads, CHUNK, q_ref, g_ref, kt_ref, st_ref, dqt_ref, own_ref, s0_ref, dp0_ref, own_slot))

    def finish(j, bias):
        rows = tile_rows(j)
        dq = (dqt_ref[:, rows] * scale).astype(dq_ref.dtype).T
        dq_ref[rows, :] = dq
        return bias + jnp.sum(dq.astype(jnp.float32).reshape(ROWS // group, group, head), axis=0)

    bias_ref[...] = lax.fori_loop(0, count_rows // ROWS, finish, jnp.zeros((group, head), jnp.float32))


def combine(scale, root, own_ref, near_ref, bias_ref, dk_ref, dv_ref, db_ref):
    head = dk_ref.shape[1]
    total = own_ref[...] + near_ref[...].astype(jnp.float32)
    dk_ref[...] = (scale * total[:, :head]).astype(dk_ref.dtype)
    dv_ref[...] = total[:, head:].astype(dv_ref.dtype)
    db_ref[...] = jnp.sum(bias_ref[...].astype(jnp.float32), axis=0) / root


SMEM = pl.BlockSpec(memory_space=pltpu.SMEM)
VMEM = pl.BlockSpec(memory_space=pltpu.VMEM)
HBM = pl.BlockSpec(memory_space=pltpu.HBM)


def call(kernel, specs, args, outs, scratch, flops):
    return pl.pallas_call(
        kernel,
        out_shape=outs,
        in_specs=specs,
        out_specs=jax.tree.map(lambda _: VMEM, outs),
        scratch_shapes=scratch,
        compiler_params=pltpu.CompilerParams(vmem_limit_bytes=VMEM_LIMIT),
        cost_estimate=pl.CostEstimate(flops=flops, bytes_accessed=4 << 20, transcendentals=0),
    )(*args)


ITEMS = pltpu.SMEM((MOST_ITEMS + 16,), jnp.int32)


def array(dtype, *shape):
    return jax.ShapeDtypeStruct(shape, dtype)


def early_part(lengths, q_hbm, g_hbm, k_hbm, v_hbm, heads):
    rows, head = q_hbm.shape
    bf16, f32 = jnp.bfloat16, jnp.float32
    return call(
        functools.partial(early_stats, heads, LOG2E / math.sqrt(head)),
        [SMEM] + [HBM] * 4,
        (lengths, q_hbm, g_hbm, k_hbm, v_hbm),
        (array(bf16, rows, head), array(bf16, rows, head), array(bf16, *k_hbm.shape), array(bf16, *k_hbm.shape),
         array(jnp.int32, 2, rows), array(f32, 3, rows), array(f32, CHUNK, ROWS), array(f32, CHUNK, ROWS)),
        [ITEMS, pltpu.SemaphoreType.DMA((6,))],
        rows * k_hbm.size * 2,
    )


def near_part(lengths, q, g, k0, v0, k1, v1, see, st, heads):
    rows, head = q.shape
    tokens = k0.shape[0]
    tiles = rows // ROWS
    own = array(jnp.float32, (tiles * (tiles + 1) // 2 - 1) * CHUNK, ROWS)
    near = array(jnp.float32, tiles * tokens, ROWS)
    return call(
        functools.partial(near_stats, heads, LOG2E / math.sqrt(head)),
        [SMEM] + [VMEM] * 8,
        (lengths, q, g, k0, v0, k1, v1, see, st),
        (array(jnp.float32, 3, rows), own, own, near, near),
        [ITEMS],
        rows * k0.size * 6,
    )


def far_part(lengths, q, g, kv2, see, st, heads):
    rows, head = q.shape
    tokens = kv2.shape[0]
    bf16, f32 = jnp.bfloat16, jnp.float32
    return call(
        functools.partial(far_grads, heads, LOG2E / math.sqrt(head)),
        [SMEM] + [VMEM] * 5,
        (lengths, q, g, kv2, see, st),
        (array(f32, 2, rows), array(bf16, tokens, 2 * head), array(f32, head, rows)),
        [pltpu.VMEM((3, rows), f32), pltpu.VMEM((tokens, 2 * head), f32), pltpu.VMEM((head, tokens), bf16),
         *(pltpu.VMEM((FAR_SLOTS * FAR_CHUNK, ROWS), f32),) * 2, ITEMS],
        rows * kv2.size,
    )


def main_part(lengths, q, g, k1, k0, kept, st, dqt, heads):
    rows, head = q.shape
    tokens = k0.shape[0]
    bf16, f32 = jnp.bfloat16, jnp.float32
    return call(
        functools.partial(main_grads, heads, 1.0 / math.sqrt(head)),
        [SMEM] + [VMEM] * 12,
        (lengths, q, g, k1, k0, *kept, st, dqt),
        (array(bf16, rows, head), array(f32, tokens, 2 * head), array(f32, tokens, 2 * head), array(f32, heads, head)),
        [pltpu.VMEM((head, rows), f32), pltpu.VMEM((head, tokens), bf16), ITEMS],
        rows * k0.size * 12,
    )


def body(queries, keys, values, output_gradient, lengths):
    tokens, heads, head = queries.shape[1:]
    rows = tokens * heads
    cp = lax.axis_size("cp")
    bf16, f32 = jnp.bfloat16, jnp.float32
    q_hbm, g_hbm, k_hbm, v_hbm = (
        pltpu.with_memory_space_constraint(x.reshape(-1, head), pltpu.HBM)
        for x in (queries, output_gradient, keys, values)
    )

    def shift(x, steps):
        return lax.ppermute(x, "cp", [(i, i + steps) for i in range(max(0, -steps), min(cp, cp - steps))])

    k1, v1 = shift(keys.reshape(tokens, head), 1), shift(values.reshape(tokens, head), 1)
    q, g, k0, v0, see, st, *early = early_part(lengths, q_hbm, g_hbm, k_hbm, v_hbm, heads)
    k1, v1, st = lax.optimization_barrier((k1, v1, st))
    kv2 = shift(jnp.concatenate([k1, v1], axis=1), 1)
    st, s0, dp0, s1, dp1 = near_part(lengths, q, g, k0, v0, k1, v1, see, st, heads)
    st, far, dqt = far_part(lengths, q, g, kv2, see, st, heads)
    far = shift(far, -1)
    dq, near, own, bias = main_part(lengths, q, g, k1, k0, (s1, dp1, *early, s0, dp0), st, dqt, heads)
    dp = lax.axis_size("dp")
    near, bias = lax.optimization_barrier(((near + far.astype(f32)).astype(bf16), bias))
    near = shift(near, -1)
    bias += sum(lax.ppermute(bias, "dp", [(i, (i + n) % dp) for i in range(dp)]) for n in range(1, dp))
    bias = lax.all_to_all(jnp.broadcast_to(bias.astype(bf16), (cp, heads, head)), "cp", 0, 0)
    root = math.sqrt(dp * cp * tokens)
    key_grad, value_grad, q_bias_grad = call(
        functools.partial(combine, 1.0 / math.sqrt(head), root),
        [VMEM] * 3,
        (own, near, bias),
        (array(bf16, tokens, head), array(bf16, tokens, head), array(f32, heads, head)),
        [],
        1000,
    )
    return (
        dq.reshape(queries.shape),
        key_grad.reshape(keys.shape),
        value_grad.reshape(values.shape),
        q_bias_grad,
    )


def solution(mesh):
    placed = (
        P("dp", "cp", "tp", None),
        P("dp", "cp", "tp", None),
        P("dp", "cp", "tp", None),
        P("dp", "cp", "tp", None),
        P("dp", None),
    )
    return jax.shard_map(
        body,
        mesh=mesh,
        in_specs=placed,
        out_specs=(
            P("dp", "cp", "tp", None),
            P("dp", "cp", "tp", None),
            P("dp", "cp", "tp", None),
            P("tp", None),
        ),
        check_vma=False,
    )
```

```python
import functools
import math

import jax
import jax.numpy as jnp
from jax import lax
from jax.experimental import pallas as pl
from jax.experimental.pallas import tpu as pltpu
from jax.sharding import PartitionSpec as P

NEGATIVE = -1e30
LOG2E = math.log2(math.e)

NT = (((1,), (1,)), ((), ()))
NN = (((1,), (0,)), ((), ()))

ROWS = 2048
CHUNK = 256
FAR_CHUNK = 128
VMEM_LIMIT = 20 << 20
MOST_ITEMS = 32
FAR_SLOTS = 4


def dot(a, b, dims):
    return lax.dot_general(a, b, dims, preferred_element_type=jnp.float32)


def block_index():
    return lax.axis_index("cp")


def doc_ends(len_ref, tokens):
    end = -block_index() * tokens
    ends = [end]
    for j in range(len_ref.shape[1]):
        end = end + len_ref[0, j]
        ends.append(end)
    return ends


def low_of(ends, pos):
    low = ends[0]
    for end in ends[1:]:
        low = jnp.where(end <= pos, end, low)
    return low


def plan(len_ref, tokens, rows, group, origin, chunk, items_ref):
    ends = doc_ends(len_ref, tokens)
    span = ROWS // group
    count = jnp.int32(0)
    for j in range(rows // ROWS):
        items_ref[MOST_ITEMS + j] = count
        t0, t1 = j * span, (j + 1) * span - 1
        low0, low1 = low_of(ends, jnp.int32(t0)), low_of(ends, jnp.int32(t1))
        begin = jnp.maximum(low0 - origin, 0) // chunk
        end = min((t1 - origin) // chunk + 1, tokens // chunk)

        def put(c, count):
            start = c * chunk + origin
            masked = (low1 > start) | (start + chunk - 1 > t0)
            items_ref[count] = j * 64 + c * 2 + masked.astype(jnp.int32)
            return count + 1

        count = lax.fori_loop(begin, end, put, count)
    return count


def each_item(items_ref, begin, end, chunk, step):
    @pl.loop(begin, end)
    def _(i):
        item = items_ref[i]
        tile = item // 64
        first = pl.multiple_of((item // 2) % 32 * chunk, chunk)

        @pl.when(item % 2 == 1)
        def _():
            step(i, tile, first, True)

        @pl.when(item % 2 == 0)
        def _():
            step(i, tile, first, False)


def each_kept(items_ref, begin, end, chunk, step):
    @pl.loop(begin, end)
    def _(i):
        item = items_ref[i]
        step(i, item // 64, pl.multiple_of((item // 2) % 32 * chunk, chunk))


def each_near(len_ref, tokens, tile, group, whole, half):
    ends = doc_ends(len_ref, tokens)
    span = ROWS // group
    low0, low1 = low_of(ends, tile * span), low_of(ends, (tile + 1) * span - 1)
    for masked in (True, False):

        @pl.when((low0 < CHUNK - tokens) & ((low1 > -tokens) == masked))
        def _():
            whole(masked)

    @pl.when((low0 >= CHUNK - tokens) & (low0 < 0))
    def _():
        half()


def tile_rows(tile):
    return pl.ds(pl.multiple_of(tile * ROWS, ROWS), ROWS)


def early_slot(i, tile, first, chunk):
    return pl.ds(0, chunk)


def own_slot(i, tile, first, chunk):
    return pl.ds(pl.multiple_of((tile * (tile + 1) // 2 - 1) * CHUNK + first, CHUNK), chunk)


def near_slot(i, tile, first, chunk):
    return pl.ds(pl.multiple_of(tile * 2 * CHUNK + first, CHUNK), chunk)


def far_slot(i, tile, first, chunk):
    return pl.ds(pl.multiple_of(i * FAR_CHUNK, FAR_CHUNK), chunk)


def hide(x, start, rows, see_ref):
    low = see_ref[0:1, rows] - start
    key = lax.broadcasted_iota(jnp.int32, x.shape, 0)
    seen = (key - low).astype(jnp.uint32) <= see_ref[1:2, rows].astype(jnp.uint32)
    return jnp.where(seen, x, NEGATIVE)


def add_stats(scale2, origin, chunk, q_ref, g_ref, k_ref, v_ref, see_ref, st_ref, s_ref, dp_ref, slot_of, i, tile, first, masked):
    rows, keys, slot = tile_rows(tile), pl.ds(first, chunk), slot_of(i, tile, first, chunk)
    scores = dot(k_ref[keys, :], q_ref[rows, :], NT) * scale2
    dprob = dot(v_ref[keys, :], g_ref[rows, :], NT)
    if masked:
        scores = hide(scores, first + origin, rows, see_ref)
    s_ref[slot, :] = scores
    dp_ref[slot, :] = dprob
    top_old = st_ref[0:1, rows]
    top = jnp.maximum(top_old, jnp.max(scores, axis=0, keepdims=True))
    expo = jnp.exp2(scores - top)
    factor = jnp.exp2(top_old - top)
    st_ref[0:1, rows] = top
    st_ref[1:2, rows] = st_ref[1:2, rows] * factor + jnp.sum(expo, axis=0, keepdims=True)
    st_ref[2:3, rows] = st_ref[2:3, rows] * factor + jnp.sum(expo * dprob, axis=0, keepdims=True)


def add_grads(chunk, q_ref, g_ref, kt_ref, st_ref, dqt_ref, sum_ref, s_ref, dp_ref, slot_of, i, tile, first):
    head = q_ref.shape[1]
    rows, keys, slot = tile_rows(tile), pl.ds(first, chunk), slot_of(i, tile, first, chunk)
    prob = jnp.exp2(s_ref[slot, :] - st_ref[0:1, rows])
    dscore = (prob * (dp_ref[slot, :] - st_ref[1:2, rows])).astype(jnp.bfloat16)
    sum_ref[keys, 0:head] += dot(dscore, q_ref[rows, :], NN)
    sum_ref[keys, head:] += dot(prob.astype(jnp.bfloat16), g_ref[rows, :], NN)
    dqt_ref[:, rows] += dot(kt_ref[:, keys], dscore, NN)


def early_stats(group, scale2, len_ref, q_hbm, g_hbm, k_hbm, v_hbm, q_ref, g_ref, k_ref, v_ref, see_ref, st_ref, s_ref, dp_ref,
                items_ref, sems):
    tokens = k_ref.shape[0]
    count_rows = q_ref.shape[0]
    fetches = [
        pltpu.make_async_copy(source, target, sems.at[n])
        for n, (source, target) in enumerate((
            (k_hbm, k_ref),
            (q_hbm.at[0:ROWS, :], q_ref.at[0:ROWS, :]),
            (v_hbm, v_ref),
            (g_hbm.at[0:ROWS, :], g_ref.at[0:ROWS, :]),
            (q_hbm.at[ROWS:, :], q_ref.at[ROWS:, :]),
            (g_hbm.at[ROWS:, :], g_ref.at[ROWS:, :]),
        ))
    ]
    for fetch in fetches:
        fetch.start()
    pos = lax.broadcasted_iota(jnp.int32, (1, count_rows), 1) // group
    low = low_of(doc_ends(len_ref, tokens), pos)
    see_ref[0:1, :] = low
    see_ref[1:2, :] = pos - low
    st_ref[0:1, :] = jnp.full((1, count_rows), NEGATIVE, jnp.float32)
    st_ref[1:3, :] = jnp.zeros((2, count_rows), jnp.float32)
    for fetch in fetches[:4]:
        fetch.wait()
    add_stats(scale2, 0, CHUNK, q_ref, g_ref, k_ref, v_ref, see_ref, st_ref, s_ref, dp_ref, early_slot, 0, 0, 0, True)
    for fetch in fetches[4:]:
        fetch.wait()


def near_stats(group, scale2, len_ref, q_ref, g_ref, k0_ref, v0_ref, k1_ref, v1_ref, see_ref, st_in,
               st_ref, s0_ref, dp0_ref, s1_ref, dp1_ref, kt0_ref, kt1_ref, items_ref):
    tokens = k0_ref.shape[0]
    st_ref[...] = st_in[...]
    kt0_ref[...] = k0_ref[...].T
    kt1_ref[...] = k1_ref[...].T
    count = plan(len_ref, tokens, q_ref.shape[0], group, 0, CHUNK, items_ref)
    each_item(items_ref, items_ref[MOST_ITEMS + 1], count, CHUNK, functools.partial(
        add_stats, scale2, 0, CHUNK, q_ref, g_ref, k0_ref, v0_ref, see_ref, st_ref, s0_ref, dp0_ref, own_slot))

    @pl.loop(0, q_ref.shape[0] // ROWS)
    def _(j):
        def add(chunk, first, masked):
            add_stats(scale2, -tokens, chunk, q_ref, g_ref, k1_ref, v1_ref, see_ref, st_ref, s1_ref, dp1_ref, near_slot,
                      0, j, first, masked)

        each_near(len_ref, tokens, j, group,
                  lambda masked: add(tokens, 0, masked), lambda: add(CHUNK, tokens - CHUNK, True))


def far_grads(group, scale2, len_ref, q_ref, g_ref, kv_ref, see_ref, st_in,
              st_ref, far_ref, dqt_ref, run_ref, sum_ref, kt_ref, s_ref, dp_ref, items_ref):
    tokens = kv_ref.shape[0]
    head = q_ref.shape[1]
    k_ref, v_ref = kv_ref.at[:, 0:head], kv_ref.at[:, head:]
    origin = -2 * tokens
    run_ref[...] = st_in[...]
    dqt_ref[...] = jnp.zeros_like(dqt_ref)
    sum_ref[...] = jnp.zeros_like(sum_ref)
    kt_ref[...] = k_ref[...].T
    count = plan(len_ref, tokens, q_ref.shape[0], group, origin, FAR_CHUNK, items_ref)
    each_item(items_ref, 0, count, FAR_CHUNK, functools.partial(
        add_stats, scale2, origin, FAR_CHUNK, q_ref, g_ref, k_ref, v_ref, see_ref, run_ref, s_ref, dp_ref, far_slot))
    total = run_ref[1:2, :]
    st_ref[0:1, :] = run_ref[0:1, :] + jnp.log2(total)
    st_ref[1:2, :] = run_ref[2:3, :] / total
    each_kept(items_ref, 0, count, FAR_CHUNK, functools.partial(
        add_grads, FAR_CHUNK, q_ref, g_ref, kt_ref, st_ref, dqt_ref, sum_ref, s_ref, dp_ref, far_slot))
    far_ref[...] = sum_ref[...].astype(far_ref.dtype)


def main_grads(group, scale, len_ref, q_ref, g_ref, kt1_ref, kt0_ref, s1_ref, dp1_ref, se_ref, dpe_ref, s0_ref, dp0_ref,
               st_ref, dqt_ref, dq_hbm, near_ref, own_ref, bias_ref, unused, dq_ref, items0_ref, sems):
    count_rows, head = q_ref.shape
    tokens = kt0_ref.shape[1]
    tiles = count_rows // ROWS
    near_ref[...] = jnp.zeros_like(near_ref)
    own_ref[...] = jnp.zeros_like(own_ref)
    bias_ref[...] = jnp.zeros_like(bias_ref)
    items0_ref[MOST_ITEMS + tiles] = plan(len_ref, tokens, count_rows, group, 0, CHUNK, items0_ref)

    def copy(j):
        return pltpu.make_async_copy(dq_ref.at[tile_rows(j), :], dq_hbm.at[tile_rows(j), :], sems.at[j])

    @pl.loop(0, tiles)
    def _(j):
        low0 = low_of(doc_ends(len_ref, tokens), j * (ROWS // group))
        for chunk, live in ((tokens, low0 < CHUNK - tokens), (CHUNK, (low0 >= CHUNK - tokens) & (low0 < 0))):

            @pl.when(live)
            def _():
                add_grads(chunk, q_ref, g_ref, kt1_ref, st_ref, dqt_ref, near_ref, s1_ref, dp1_ref, near_slot,
                          0, j, tokens - chunk)

        @pl.when(j == 0)
        def _():
            add_grads(CHUNK, q_ref, g_ref, kt0_ref, st_ref, dqt_ref, own_ref, se_ref, dpe_ref, early_slot, 0, 0, 0)

        @pl.when(j > 0)
        def _():
            each_kept(items0_ref, items0_ref[MOST_ITEMS + j], items0_ref[MOST_ITEMS + j + 1], CHUNK, functools.partial(
                add_grads, CHUNK, q_ref, g_ref, kt0_ref, st_ref, dqt_ref, own_ref, s0_ref, dp0_ref, own_slot))

        rows = tile_rows(j)
        dq = (dqt_ref[:, rows] * scale).astype(dq_ref.dtype).T
        dq_ref[rows, :] = dq
        copy(j).start()
        bias_ref[...] += jnp.sum(dq.astype(jnp.float32).reshape(ROWS // group, group, head), axis=0)

    for j in range(tiles):
        copy(j).wait()


def combine(scale, root, own_ref, near_ref, bias_ref, dk_ref, dv_ref, db_ref):
    head = dk_ref.shape[1]
    total = own_ref[...] + near_ref[...].astype(jnp.float32)
    dk_ref[...] = (scale * total[:, :head]).astype(dk_ref.dtype)
    dv_ref[...] = total[:, head:].astype(dv_ref.dtype)
    db_ref[...] = jnp.sum(bias_ref[...].astype(jnp.float32), axis=0) / root


SMEM = pl.BlockSpec(memory_space=pltpu.SMEM)
VMEM = pl.BlockSpec(memory_space=pltpu.VMEM)
HBM = pl.BlockSpec(memory_space=pltpu.HBM)


def call(kernel, specs, args, outs, scratch, flops, out_specs=None, aliases={}):
    return pl.pallas_call(
        kernel,
        out_shape=outs,
        in_specs=specs,
        out_specs=out_specs or jax.tree.map(lambda _: VMEM, outs),
        input_output_aliases=aliases,
        scratch_shapes=scratch,
        compiler_params=pltpu.CompilerParams(vmem_limit_bytes=VMEM_LIMIT),
        cost_estimate=pl.CostEstimate(flops=flops, bytes_accessed=4 << 20, transcendentals=0),
    )(*args)


ITEMS = pltpu.SMEM((MOST_ITEMS + 16,), jnp.int32)


def array(dtype, *shape):
    return jax.ShapeDtypeStruct(shape, dtype)


def early_part(lengths, q_hbm, g_hbm, k_hbm, v_hbm, heads):
    rows, head = q_hbm.shape
    bf16, f32 = jnp.bfloat16, jnp.float32
    return call(
        functools.partial(early_stats, heads, LOG2E / math.sqrt(head)),
        [SMEM] + [HBM] * 4,
        (lengths, q_hbm, g_hbm, k_hbm, v_hbm),
        (array(bf16, rows, head), array(bf16, rows, head), array(bf16, *k_hbm.shape), array(bf16, *k_hbm.shape),
         array(jnp.int32, 2, rows), array(f32, 3, rows), array(f32, CHUNK, ROWS), array(f32, CHUNK, ROWS)),
        [ITEMS, pltpu.SemaphoreType.DMA((6,))],
        rows * k_hbm.size * 2,
    )


def near_part(lengths, q, g, k0, v0, k1, v1, see, st, heads):
    rows, head = q.shape
    tokens = k0.shape[0]
    tiles = rows // ROWS
    own = array(jnp.float32, (tiles * (tiles + 1) // 2 - 1) * CHUNK, ROWS)
    near = array(jnp.float32, tiles * tokens, ROWS)
    return call(
        functools.partial(near_stats, heads, LOG2E / math.sqrt(head)),
        [SMEM] + [VMEM] * 8,
        (lengths, q, g, k0, v0, k1, v1, see, st),
        (array(jnp.float32, 3, rows), own, own, near, near, array(k0.dtype, head, tokens), array(k0.dtype, head, tokens)),
        [ITEMS],
        rows * k0.size * 6,
    )


def far_part(lengths, q, g, kv2, see, st, heads):
    rows, head = q.shape
    tokens = kv2.shape[0]
    bf16, f32 = jnp.bfloat16, jnp.float32
    return call(
        functools.partial(far_grads, heads, LOG2E / math.sqrt(head)),
        [SMEM] + [VMEM] * 5,
        (lengths, q, g, kv2, see, st),
        (array(f32, 2, rows), array(bf16, tokens, 2 * head), array(f32, head, rows)),
        [pltpu.VMEM((3, rows), f32), pltpu.VMEM((tokens, 2 * head), f32), pltpu.VMEM((head, tokens), bf16),
         *(pltpu.VMEM((FAR_SLOTS * FAR_CHUNK, ROWS), f32),) * 2, ITEMS],
        rows * kv2.size,
    )


def main_part(lengths, q, g, kt1, kt0, kept, st, dqt, heads):
    rows, head = q.shape
    tokens = kt0.shape[1]
    bf16, f32 = jnp.bfloat16, jnp.float32
    return call(
        functools.partial(main_grads, heads, 1.0 / math.sqrt(head)),
        [SMEM] + [VMEM] * 12,
        (lengths, q, g, kt1, kt0, *kept, st, dqt),
        (array(bf16, rows, head), array(f32, tokens, 2 * head), array(f32, tokens, 2 * head), array(f32, heads, head),
         array(f32, *dqt.shape)),
        [pltpu.VMEM((rows, head), bf16), ITEMS, pltpu.SemaphoreType.DMA((rows // ROWS,))],
        rows * tokens * head * 12,
        out_specs=(HBM, VMEM, VMEM, VMEM, VMEM),
        aliases={12: 4},
    )[:4]


def body(queries, keys, values, output_gradient, lengths):
    tokens, heads, head = queries.shape[1:]
    rows = tokens * heads
    cp = lax.axis_size("cp")
    bf16, f32 = jnp.bfloat16, jnp.float32
    q_hbm, g_hbm, k_hbm, v_hbm = (
        pltpu.with_memory_space_constraint(x.reshape(-1, head), pltpu.HBM)
        for x in (queries, output_gradient, keys, values)
    )

    def shift(x, steps):
        return lax.ppermute(x, "cp", [(i, i + steps) for i in range(max(0, -steps), min(cp, cp - steps))])

    k1, v1 = shift(keys.reshape(tokens, head), 1), shift(values.reshape(tokens, head), 1)
    q, g, k0, v0, see, st, *early = early_part(lengths, q_hbm, g_hbm, k_hbm, v_hbm, heads)
    k1, v1, st = lax.optimization_barrier((k1, v1, st))
    kv2 = shift(jnp.concatenate([k1, v1], axis=1), 1)
    st, s0, dp0, s1, dp1, kt0, kt1 = near_part(lengths, q, g, k0, v0, k1, v1, see, st, heads)
    st, far, dqt = far_part(lengths, q, g, kv2, see, st, heads)
    far = shift(far, -1)
    dq, near, own, bias = main_part(lengths, q, g, kt1, kt0, (s1, dp1, *early, s0, dp0), st, dqt, heads)
    dp = lax.axis_size("dp")
    near, bias = lax.optimization_barrier(((near + far.astype(f32)).astype(bf16), bias))
    near = shift(near, -1)
    bias += sum(lax.ppermute(bias, "dp", [(i, (i + n) % dp) for i in range(dp)]) for n in range(1, dp))
    bias = lax.all_to_all(jnp.broadcast_to(bias.astype(bf16), (cp, heads, head)), "cp", 0, 0)
    root = math.sqrt(dp * cp * tokens)
    key_grad, value_grad, q_bias_grad = call(
        functools.partial(combine, 1.0 / math.sqrt(head), root),
        [VMEM] * 3,
        (own, near, bias),
        (array(bf16, tokens, head), array(bf16, tokens, head), array(f32, heads, head)),
        [],
        1000,
    )
    return (
        dq.reshape(queries.shape),
        key_grad.reshape(keys.shape),
        value_grad.reshape(values.shape),
        q_bias_grad,
    )


def solution(mesh):
    placed = (
        P("dp", "cp", "tp", None),
        P("dp", "cp", "tp", None),
        P("dp", "cp", "tp", None),
        P("dp", "cp", "tp", None),
        P("dp", None),
    )
    return jax.shard_map(
        body,
        mesh=mesh,
        in_specs=placed,
        out_specs=(
            P("dp", "cp", "tp", None),
            P("dp", "cp", "tp", None),
            P("dp", "cp", "tp", None),
            P("tp", None),
        ),
        check_vma=False,
    )
```

```python
import functools
import math

import jax
import jax.numpy as jnp
from jax import lax
from jax.experimental import pallas as pl
from jax.experimental.pallas import tpu as pltpu
from jax.sharding import PartitionSpec as P

NEGATIVE = -1e30
LOG2E = math.log2(math.e)

NT = (((1,), (1,)), ((), ()))
NN = (((1,), (0,)), ((), ()))

ROWS = 2048
CHUNK = 256
FAR_CHUNK = 128
VMEM_LIMIT = 20 << 20
MOST_ITEMS = 32
FAR_SLOTS = 4


def dot(a, b, dims):
    return lax.dot_general(a, b, dims, preferred_element_type=jnp.float32)


def block_index():
    return lax.axis_index("cp")


def doc_ends(len_ref, tokens):
    end = -block_index() * tokens
    ends = [end]
    for j in range(len_ref.shape[1]):
        end = end + len_ref[0, j]
        ends.append(end)
    return ends


def low_of(ends, pos):
    low = ends[0]
    for end in ends[1:]:
        low = jnp.where(end <= pos, end, low)
    return low


def plan(len_ref, tokens, rows, group, origin, chunk, items_ref):
    ends = doc_ends(len_ref, tokens)
    span = ROWS // group
    count = jnp.int32(0)
    for j in range(rows // ROWS):
        items_ref[MOST_ITEMS + j] = count
        t0, t1 = j * span, (j + 1) * span - 1
        low0, low1 = low_of(ends, jnp.int32(t0)), low_of(ends, jnp.int32(t1))
        begin = jnp.maximum(low0 - origin, 0) // chunk
        end = min((t1 - origin) // chunk + 1, tokens // chunk)

        def put(c, count):
            start = c * chunk + origin
            masked = (low1 > start) | (start + chunk - 1 > t0)
            items_ref[count] = j * 64 + c * 2 + masked.astype(jnp.int32)
            return count + 1

        count = lax.fori_loop(begin, end, put, count)
    return count


def each_item(items_ref, begin, end, chunk, step):
    @pl.loop(begin, end)
    def _(i):
        item = items_ref[i]
        tile = item // 64
        first = pl.multiple_of((item // 2) % 32 * chunk, chunk)

        @pl.when(item % 2 == 1)
        def _():
            step(i, tile, first, True)

        @pl.when(item % 2 == 0)
        def _():
            step(i, tile, first, False)


def each_kept(items_ref, begin, end, chunk, step):
    @pl.loop(begin, end)
    def _(i):
        item = items_ref[i]
        step(i, item // 64, pl.multiple_of((item // 2) % 32 * chunk, chunk))


def each_near(len_ref, tokens, tile, group, whole, half):
    ends = doc_ends(len_ref, tokens)
    span = ROWS // group
    low0, low1 = low_of(ends, tile * span), low_of(ends, (tile + 1) * span - 1)
    for masked in (True, False):

        @pl.when((low0 < CHUNK - tokens) & ((low1 > -tokens) == masked))
        def _():
            whole(masked)

    @pl.when((low0 >= CHUNK - tokens) & (low0 < 0))
    def _():
        half()


def tile_rows(tile):
    return pl.ds(pl.multiple_of(tile * ROWS, ROWS), ROWS)


def early_slot(i, tile, first, chunk):
    return pl.ds(0, chunk)


def own_slot(i, tile, first, chunk):
    return pl.ds(pl.multiple_of((tile * (tile + 1) // 2 - 1) * CHUNK + first, CHUNK), chunk)


def near_slot(i, tile, first, chunk):
    return pl.ds(pl.multiple_of(tile * 2 * CHUNK + first, CHUNK), chunk)


def far_slot(i, tile, first, chunk):
    return pl.ds(pl.multiple_of(i * FAR_CHUNK, FAR_CHUNK), chunk)


def plan_far(len_ref, tokens, rows, group, items_ref):
    ends = doc_ends(len_ref, tokens)
    span = ROWS // group
    count, slot = jnp.int32(0), jnp.int32(0)
    for j in range(rows // ROWS):
        low0, low1 = low_of(ends, jnp.int32(j * span)), low_of(ends, jnp.int32((j + 1) * span - 1))
        begin = jnp.maximum(low0 + 2 * tokens, 0) // FAR_CHUNK
        for last in range(1, tokens // FAR_CHUNK, 2):
            double = (begin < last).astype(jnp.int32)
            chunk = last - double
            masked = (low1 > chunk * FAR_CHUNK - 2 * tokens).astype(jnp.int32)
            live = (begin <= last).astype(jnp.int32)
            items_ref[count] = slot * 1024 + double * 512 + j * 64 + chunk * 2 + masked
            count += live
            slot += live * (1 + double)
    return count


def each_far(items_ref, count, step):
    @pl.loop(0, count)
    def _(i):
        item = items_ref[i]
        slot, tile = item // 1024, (item // 64) % 8
        first = pl.multiple_of((item // 2) % 32 * FAR_CHUNK, FAR_CHUNK)
        for double in (0, 1):

            @pl.when((item // 512) % 2 == double)
            def _():
                step(slot, tile, first, (1 + double) * FAR_CHUNK, item % 2)


def hide(x, start, rows, see_ref):
    low = see_ref[0:1, rows] - start
    key = lax.broadcasted_iota(jnp.int32, x.shape, 0)
    seen = (key - low).astype(jnp.uint32) <= see_ref[1:2, rows].astype(jnp.uint32)
    return jnp.where(seen, x, NEGATIVE)


def add_stats(scale2, origin, chunk, q_ref, g_ref, k_ref, v_ref, see_ref, st_ref, s_ref, dp_ref, slot_of, i, tile, first, masked):
    rows, keys, slot = tile_rows(tile), pl.ds(first, chunk), slot_of(i, tile, first, chunk)
    scores = dot(k_ref[keys, :], q_ref[rows, :], NT) * scale2
    dprob = dot(v_ref[keys, :], g_ref[rows, :], NT)
    if masked:
        scores = hide(scores, first + origin, rows, see_ref)
    s_ref[slot, :] = scores
    dp_ref[slot, :] = dprob
    top_old = st_ref[0:1, rows]
    top = jnp.maximum(top_old, jnp.max(scores, axis=0, keepdims=True))
    expo = jnp.exp2(scores - top)
    factor = jnp.exp2(top_old - top)
    st_ref[0:1, rows] = top
    st_ref[1:2, rows] = st_ref[1:2, rows] * factor + jnp.sum(expo, axis=0, keepdims=True)
    st_ref[2:3, rows] = st_ref[2:3, rows] * factor + jnp.sum(expo * dprob, axis=0, keepdims=True)


def add_grads(chunk, q_ref, g_ref, kt_ref, st_ref, dqt_ref, sum_ref, s_ref, dp_ref, slot_of, i, tile, first):
    head = q_ref.shape[1]
    rows, keys, slot = tile_rows(tile), pl.ds(first, chunk), slot_of(i, tile, first, chunk)
    prob = jnp.exp2(s_ref[slot, :] - st_ref[0:1, rows])
    dscore = (prob * (dp_ref[slot, :] - st_ref[1:2, rows])).astype(jnp.bfloat16)
    sum_ref[keys, 0:head] += dot(dscore, q_ref[rows, :], NN)
    sum_ref[keys, head:] += dot(prob.astype(jnp.bfloat16), g_ref[rows, :], NN)
    dqt_ref[:, rows] += dot(kt_ref[:, keys], dscore, NN)


def early_stats(group, scale2, len_ref, q_hbm, g_hbm, k_hbm, v_hbm, q_ref, g_ref, k_ref, v_ref, see_ref, st_ref, s_ref, dp_ref,
                items_ref, sems):
    tokens = k_ref.shape[0]
    count_rows = q_ref.shape[0]
    fetches = [
        pltpu.make_async_copy(source, target, sems.at[n])
        for n, (source, target) in enumerate((
            (k_hbm, k_ref),
            (q_hbm.at[0:ROWS, :], q_ref.at[0:ROWS, :]),
            (v_hbm, v_ref),
            (g_hbm.at[0:ROWS, :], g_ref.at[0:ROWS, :]),
            (q_hbm.at[ROWS:, :], q_ref.at[ROWS:, :]),
            (g_hbm.at[ROWS:, :], g_ref.at[ROWS:, :]),
        ))
    ]
    for fetch in fetches:
        fetch.start()
    pos = lax.broadcasted_iota(jnp.int32, (1, count_rows), 1) // group
    low = low_of(doc_ends(len_ref, tokens), pos)
    see_ref[0:1, :] = low
    see_ref[1:2, :] = pos - low
    st_ref[0:1, :] = jnp.full((1, count_rows), NEGATIVE, jnp.float32)
    st_ref[1:3, :] = jnp.zeros((2, count_rows), jnp.float32)
    for fetch in fetches[:4]:
        fetch.wait()
    add_stats(scale2, 0, CHUNK, q_ref, g_ref, k_ref, v_ref, see_ref, st_ref, s_ref, dp_ref, early_slot, 0, 0, 0, True)
    for fetch in fetches[4:]:
        fetch.wait()


def near_stats(group, scale2, len_ref, q_ref, g_ref, k0_ref, v0_ref, k1_ref, v1_ref, see_ref, st_in,
               st_ref, s0_ref, dp0_ref, s1_ref, dp1_ref, kt0_ref, kt1_ref, items_ref):
    tokens = k0_ref.shape[0]
    st_ref[...] = st_in[...]
    kt0_ref[...] = k0_ref[...].T
    kt1_ref[...] = k1_ref[...].T
    count = plan(len_ref, tokens, q_ref.shape[0], group, 0, CHUNK, items_ref)
    each_item(items_ref, items_ref[MOST_ITEMS + 1], count, CHUNK, functools.partial(
        add_stats, scale2, 0, CHUNK, q_ref, g_ref, k0_ref, v0_ref, see_ref, st_ref, s0_ref, dp0_ref, own_slot))

    @pl.loop(0, q_ref.shape[0] // ROWS)
    def _(j):
        def add(chunk, first, masked):
            add_stats(scale2, -tokens, chunk, q_ref, g_ref, k1_ref, v1_ref, see_ref, st_ref, s1_ref, dp1_ref, near_slot,
                      0, j, first, masked)

        each_near(len_ref, tokens, j, group,
                  lambda masked: add(tokens, 0, masked), lambda: add(CHUNK, tokens - CHUNK, True))


def far_grads(group, scale2, len_ref, q_ref, g_ref, kv_ref, see_ref, st_in,
              st_ref, far_ref, dqt_ref, run_ref, sum_ref, kt_ref, s_ref, dp_ref, items_ref):
    tokens = kv_ref.shape[0]
    head = q_ref.shape[1]
    k_ref, v_ref = kv_ref.at[:, 0:head], kv_ref.at[:, head:]
    origin = -2 * tokens
    run_ref[...] = st_in[...]
    dqt_ref[...] = jnp.zeros_like(dqt_ref)
    sum_ref[...] = jnp.zeros_like(sum_ref)
    kt_ref[...] = k_ref[...].T
    count = plan_far(len_ref, tokens, q_ref.shape[0], group, items_ref)

    def add(slot, tile, first, chunk, masked):
        for hidden in (0, 1):

            @pl.when(masked == hidden)
            def _():
                add_stats(scale2, origin, chunk, q_ref, g_ref, k_ref, v_ref, see_ref, run_ref, s_ref, dp_ref, far_slot,
                          slot, tile, first, hidden == 1)

    each_far(items_ref, count, add)
    total = run_ref[1:2, :]
    st_ref[0:1, :] = run_ref[0:1, :] + jnp.log2(total)
    st_ref[1:2, :] = run_ref[2:3, :] / total
    each_far(items_ref, count, lambda slot, tile, first, chunk, masked: add_grads(
        chunk, q_ref, g_ref, kt_ref, st_ref, dqt_ref, sum_ref, s_ref, dp_ref, far_slot, slot, tile, first))
    far_ref[...] = sum_ref[...].astype(far_ref.dtype)


def main_grads(group, scale, len_ref, q_ref, g_ref, kt1_ref, kt0_ref, s1_ref, dp1_ref, se_ref, dpe_ref, s0_ref, dp0_ref,
               st_ref, dqt_ref, dq_hbm, near_ref, own_ref, bias_ref, unused, dq_ref, items0_ref, sems):
    count_rows, head = q_ref.shape
    tokens = kt0_ref.shape[1]
    tiles = count_rows // ROWS
    near_ref[...] = jnp.zeros_like(near_ref)
    own_ref[...] = jnp.zeros_like(own_ref)
    bias_ref[...] = jnp.zeros_like(bias_ref)
    items0_ref[MOST_ITEMS + tiles] = plan(len_ref, tokens, count_rows, group, 0, CHUNK, items0_ref)

    def copy(j):
        return pltpu.make_async_copy(dq_ref.at[tile_rows(j), :], dq_hbm.at[tile_rows(j), :], sems.at[j])

    @pl.loop(0, tiles)
    def _(j):
        low0 = low_of(doc_ends(len_ref, tokens), j * (ROWS // group))
        for chunk, live in ((tokens, low0 < CHUNK - tokens), (CHUNK, (low0 >= CHUNK - tokens) & (low0 < 0))):

            @pl.when(live)
            def _():
                add_grads(chunk, q_ref, g_ref, kt1_ref, st_ref, dqt_ref, near_ref, s1_ref, dp1_ref, near_slot,
                          0, j, tokens - chunk)

        @pl.when(j == 0)
        def _():
            add_grads(CHUNK, q_ref, g_ref, kt0_ref, st_ref, dqt_ref, own_ref, se_ref, dpe_ref, early_slot, 0, 0, 0)

        @pl.when(j > 0)
        def _():
            each_kept(items0_ref, items0_ref[MOST_ITEMS + j], items0_ref[MOST_ITEMS + j + 1], CHUNK, functools.partial(
                add_grads, CHUNK, q_ref, g_ref, kt0_ref, st_ref, dqt_ref, own_ref, s0_ref, dp0_ref, own_slot))

        rows = tile_rows(j)
        dq = (dqt_ref[:, rows] * scale).astype(dq_ref.dtype).T
        dq_ref[rows, :] = dq
        copy(j).start()
        bias_ref[...] += jnp.sum(dq.astype(jnp.float32).reshape(ROWS // group, group, head), axis=0)

    for j in range(tiles):
        copy(j).wait()


def combine(scale, root, own_ref, near_ref, bias_ref, dk_ref, dv_ref, db_ref):
    head = dk_ref.shape[1]
    total = own_ref[...] + near_ref[...].astype(jnp.float32)
    dk_ref[...] = (scale * total[:, :head]).astype(dk_ref.dtype)
    dv_ref[...] = total[:, head:].astype(dv_ref.dtype)
    db_ref[...] = jnp.sum(bias_ref[...].astype(jnp.float32), axis=0) / root


SMEM = pl.BlockSpec(memory_space=pltpu.SMEM)
VMEM = pl.BlockSpec(memory_space=pltpu.VMEM)
HBM = pl.BlockSpec(memory_space=pltpu.HBM)


def call(kernel, specs, args, outs, scratch, flops, out_specs=None, aliases={}):
    return pl.pallas_call(
        kernel,
        out_shape=outs,
        in_specs=specs,
        out_specs=out_specs or jax.tree.map(lambda _: VMEM, outs),
        input_output_aliases=aliases,
        scratch_shapes=scratch,
        compiler_params=pltpu.CompilerParams(vmem_limit_bytes=VMEM_LIMIT),
        cost_estimate=pl.CostEstimate(flops=flops, bytes_accessed=4 << 20, transcendentals=0),
    )(*args)


ITEMS = pltpu.SMEM((MOST_ITEMS + 16,), jnp.int32)


def array(dtype, *shape):
    return jax.ShapeDtypeStruct(shape, dtype)


def early_part(lengths, q_hbm, g_hbm, k_hbm, v_hbm, heads):
    rows, head = q_hbm.shape
    bf16, f32 = jnp.bfloat16, jnp.float32
    return call(
        functools.partial(early_stats, heads, LOG2E / math.sqrt(head)),
        [SMEM] + [HBM] * 4,
        (lengths, q_hbm, g_hbm, k_hbm, v_hbm),
        (array(bf16, rows, head), array(bf16, rows, head), array(bf16, *k_hbm.shape), array(bf16, *k_hbm.shape),
         array(jnp.int32, 2, rows), array(f32, 3, rows), array(f32, CHUNK, ROWS), array(f32, CHUNK, ROWS)),
        [ITEMS, pltpu.SemaphoreType.DMA((6,))],
        rows * k_hbm.size * 2,
    )


def near_part(lengths, q, g, k0, v0, k1, v1, see, st, heads):
    rows, head = q.shape
    tokens = k0.shape[0]
    tiles = rows // ROWS
    own = array(jnp.float32, (tiles * (tiles + 1) // 2 - 1) * CHUNK, ROWS)
    near = array(jnp.float32, tiles * tokens, ROWS)
    return call(
        functools.partial(near_stats, heads, LOG2E / math.sqrt(head)),
        [SMEM] + [VMEM] * 8,
        (lengths, q, g, k0, v0, k1, v1, see, st),
        (array(jnp.float32, 3, rows), own, own, near, near, array(k0.dtype, head, tokens), array(k0.dtype, head, tokens)),
        [ITEMS],
        rows * k0.size * 6,
    )


def far_part(lengths, q, g, kv2, see, st, heads):
    rows, head = q.shape
    tokens = kv2.shape[0]
    bf16, f32 = jnp.bfloat16, jnp.float32
    return call(
        functools.partial(far_grads, heads, LOG2E / math.sqrt(head)),
        [SMEM] + [VMEM] * 5,
        (lengths, q, g, kv2, see, st),
        (array(f32, 2, rows), array(bf16, tokens, 2 * head), array(f32, head, rows)),
        [pltpu.VMEM((3, rows), f32), pltpu.VMEM((tokens, 2 * head), f32), pltpu.VMEM((head, tokens), bf16),
         *(pltpu.VMEM((FAR_SLOTS * FAR_CHUNK, ROWS), f32),) * 2, ITEMS],
        rows * kv2.size,
    )


def main_part(lengths, q, g, kt1, kt0, kept, st, dqt, heads):
    rows, head = q.shape
    tokens = kt0.shape[1]
    bf16, f32 = jnp.bfloat16, jnp.float32
    return call(
        functools.partial(main_grads, heads, 1.0 / math.sqrt(head)),
        [SMEM] + [VMEM] * 12,
        (lengths, q, g, kt1, kt0, *kept, st, dqt),
        (array(bf16, rows, head), array(f32, tokens, 2 * head), array(f32, tokens, 2 * head), array(f32, heads, head),
         array(f32, *dqt.shape)),
        [pltpu.VMEM((rows, head), bf16), ITEMS, pltpu.SemaphoreType.DMA((rows // ROWS,))],
        rows * tokens * head * 12,
        out_specs=(HBM, VMEM, VMEM, VMEM, VMEM),
        aliases={12: 4},
    )[:4]


def body(queries, keys, values, output_gradient, lengths):
    tokens, heads, head = queries.shape[1:]
    rows = tokens * heads
    cp = lax.axis_size("cp")
    bf16, f32 = jnp.bfloat16, jnp.float32
    q_hbm, g_hbm, k_hbm, v_hbm = (
        pltpu.with_memory_space_constraint(x.reshape(-1, head), pltpu.HBM)
        for x in (queries, output_gradient, keys, values)
    )

    def shift(x, steps):
        return lax.ppermute(x, "cp", [(i, i + steps) for i in range(max(0, -steps), min(cp, cp - steps))])

    k1, v1 = shift(keys.reshape(tokens, head), 1), shift(values.reshape(tokens, head), 1)
    q, g, k0, v0, see, st, *early = early_part(lengths, q_hbm, g_hbm, k_hbm, v_hbm, heads)
    k1, v1, st = lax.optimization_barrier((k1, v1, st))
    kv2 = shift(jnp.concatenate([k1, v1], axis=1), 1)
    st, s0, dp0, s1, dp1, kt0, kt1 = near_part(lengths, q, g, k0, v0, k1, v1, see, st, heads)
    st, far, dqt = far_part(lengths, q, g, kv2, see, st, heads)
    far = shift(far, -1)
    dq, near, own, bias = main_part(lengths, q, g, kt1, kt0, (s1, dp1, *early, s0, dp0), st, dqt, heads)
    dp = lax.axis_size("dp")
    near, bias = lax.optimization_barrier(((near + far.astype(f32)).astype(bf16), bias))
    near = shift(near, -1)
    bias += sum(lax.ppermute(bias, "dp", [(i, (i + n) % dp) for i in range(dp)]) for n in range(1, dp))
    bias = lax.all_to_all(jnp.broadcast_to(bias.astype(bf16), (cp, heads, head)), "cp", 0, 0)
    root = math.sqrt(dp * cp * tokens)
    key_grad, value_grad, q_bias_grad = call(
        functools.partial(combine, 1.0 / math.sqrt(head), root),
        [VMEM] * 3,
        (own, near, bias),
        (array(bf16, tokens, head), array(bf16, tokens, head), array(f32, heads, head)),
        [],
        1000,
    )
    return (
        dq.reshape(queries.shape),
        key_grad.reshape(keys.shape),
        value_grad.reshape(values.shape),
        q_bias_grad,
    )


def solution(mesh):
    placed = (
        P("dp", "cp", "tp", None),
        P("dp", "cp", "tp", None),
        P("dp", "cp", "tp", None),
        P("dp", "cp", "tp", None),
        P("dp", None),
    )
    return jax.shard_map(
        body,
        mesh=mesh,
        in_specs=placed,
        out_specs=(
            P("dp", "cp", "tp", None),
            P("dp", "cp", "tp", None),
            P("dp", "cp", "tp", None),
            P("tp", None),
        ),
        check_vma=False,
    )
```
